32 devices in a mesh: groups: 2 (over y), seq: 4 (over z), section: 2 (over x), chan: 2 (over core).
Axes of the slice: x: 2, y: 2, z: 4, core: 2. Of those that a mesh axis runs over, the one named last changes fastest.
Arguments:
- base_codes: int32 [131072], P(('groups', 'seq', 'section')), parts along dimension 0, may hold values from 0 to 3
- stem_weight: bfloat16 [64, 768], replicated, as said below
- conv_gain: float32 [768], replicated, may hold values from 0.1 to 1.9
- dilated_conv_weight: bfloat16 [3, 768, 768], P(None, None, 'chan'), may hold values from -0.125 to 0.125
- widen_weight: bfloat16 [768, 1536], P(None, 'chan'), may hold values from -0.21875 to 0.21875
- token_gain: float32 [1536], replicated, may hold values from 0.1 to 1.9
- proj_weight: bfloat16 [1536, 256], replicated, may hold values from -0.15625 to 0.15625
- dist_weight: float32 [128], replicated, may hold values from -4 to 4
- pair_weight_one: bfloat16 [3, 3, 128, 128], P(None, None, None, 'chan'), may hold values from -0.1875 to 0.1875
- pair_weight_two: bfloat16 [3, 3, 128, 128], P(None, None, None, 'chan'), may hold values from -0.1875 to 0.1875
Outputs:
- fine_features: bfloat16 [4096, 1536], P(('groups', 'seq', 'section'), 'chan'), parts along dimension 0
- pair_map: bfloat16 [128, 64, 32], P('chan', ('groups', 'seq'), 'section'), parts along dimension 1
The draws below stay inside these ranges and needn't reach their ends.
There are 2 independent parts, one for each index of `groups`. The reference program is written for one: setup_inputs(seed, part) draws one part's arguments, and reference() takes and returns one part's arrays. A program takes and returns all parts, laid end to end along the dimension named above; an argument that names none is the same for every part. Nothing has to cross between parts.
Inputs may be any that keep to these rules, and one draw needn't show every extreme that they name: Each entry of stem_weight is under 9 / sqrt(16) in magnitude.
All inputs are finite; a program needn't handle non-finite values.
Results may differ from the reference program's by a relative error of at most 0.015.
Values may be sent and summed in bfloat16 or wider, within the bound.
A program may use at most 64 MiB of HBM per device.

```python
import math
import jax
import jax.numpy as jnp
from jax import lax

C1 = 768
C2 = 1536
PC = 128
PATCH = 16
POOL = 64
DILATION_ROWS = 4
TOKENS = 32
BASES = 65536


def draw_stem_weight(key, part):
    key_base = jax.random.fold_in(key, 11)
    key_scale = jax.random.fold_in(key, 12)
    exponent = jax.random.uniform(key_scale, (C1,), jnp.float32)
    column_scale = 0.22 * jnp.exp(exponent * math.log(10.0))
    values = jnp.clip(jax.random.normal(key_base, (4 * PATCH, C1), jnp.float32), -4.0, 4.0)
    return (values * column_scale[None, :] / math.sqrt(PATCH)).astype(jnp.bfloat16)


def place_ends(drawn, stream_key, smallest, high):
    spot = [jax.random.randint(jax.random.fold_in(stream_key, axis), (), 0, length) for axis, length in enumerate(drawn.shape)]
    longest = drawn.shape.index(max(drawn.shape))
    beside = spot[:longest] + [(spot[longest] + 1) % drawn.shape[longest]] + spot[longest + 1:]
    return drawn.at[tuple(spot)].set(smallest).at[tuple(beside)].set(high)


def shard_levels(key, shape, split, low, high):
    def one(dim, blocks):
        draws = jax.random.uniform(jax.random.fold_in(jax.random.fold_in(key, 6), dim), (blocks,), jnp.float32, low / len(split), high / len(split))
        return jnp.repeat(jnp.exp(draws), shape[dim] // blocks).reshape((-1,) + (1,) * (len(shape) - dim - 1))

    level = one(*split[0])
    for cut in split[1:]:
        level = level * one(*cut)
    return level


def gaussian(key, dims, width, most, split=(), kind=jnp.bfloat16):
    drawn = width * jax.random.normal(key, dims, jnp.float32)
    if split:
        drawn = drawn * shard_levels(key, dims, split, -0.22, 0.18)
    return jnp.clip(drawn, -most, most).astype(kind)


def setup_inputs(seed: int = 0, part: int = 0) -> dict:
    seeds = jax.random.split(jax.random.key(seed), 11)
    part_keys = jax.random.split(jax.random.fold_in(seeds[10], part), 11)
    base_codes = place_ends(jax.random.randint(part_keys[0], (BASES,), 0, 4), jax.random.fold_in(part_keys[0], 1), 0, 3).astype(jnp.int32)
    stem_weight = draw_stem_weight(jax.random.fold_in(seeds[10], 71), part)
    conv_gain = jnp.clip(1.0 + 0.18 * jax.random.normal(seeds[2], (C1,), jnp.float32), 0.1, 1.9)
    dilated_conv_weight = gaussian(seeds[3], (3, C1, C1), (3 * C1) ** -0.5, 0.125, ((2, 2),))
    widen_weight = gaussian(seeds[4], (C1, C2), C1 ** -0.5, 0.21875, ((1, 2),))
    token_gain = jnp.clip(1.0 + 0.18 * jax.random.normal(seeds[5], (C2,), jnp.float32), 0.1, 1.9)
    proj_weight = gaussian(seeds[6], (C2, 2 * PC), C2 ** -0.5, 0.15625)
    dist_weight = gaussian(seeds[7], (PC,), 1.0, 4.0, (), jnp.float32)
    pair_weight_one = gaussian(seeds[8], (3, 3, PC, PC), (9 * PC) ** -0.5, 0.1875, ((3, 2),))
    pair_weight_two = gaussian(seeds[9], (3, 3, PC, PC), (9 * PC) ** -0.5, 0.1875, ((3, 2),))
    return {"base_codes": base_codes, "stem_weight": stem_weight, "conv_gain": conv_gain, "dilated_conv_weight": dilated_conv_weight, "widen_weight": widen_weight, "token_gain": token_gain, "proj_weight": proj_weight, "dist_weight": dist_weight, "pair_weight_one": pair_weight_one, "pair_weight_two": pair_weight_two}


epsilon = 1e-06

def row_norm(values, gain):
    mean_square = lax.optimization_barrier(jnp.mean(values * values, axis=1, keepdims=True))
    return values * lax.rsqrt(mean_square + epsilon) * gain

def pair_conv(active, weight):
    padded_rows = jnp.pad(active, ((0, 0), (1, 1), (1, 1)))
    row_len = active.shape[1]
    col_len = active.shape[2]
    total = jnp.zeros((weight.shape[3], row_len, col_len), jnp.float32)
    for shift_row in range(3):
        for shift_col in range(3):
            window = padded_rows[:, shift_row:shift_row + row_len, shift_col:shift_col + col_len].astype(jnp.float32)
            total = total + jnp.einsum('co,crs->ors', weight[shift_row, shift_col].astype(jnp.float32), window)
    return total

def reference(base_codes, stem_weight, conv_gain, dilated_conv_weight, widen_weight, token_gain, proj_weight, dist_weight, pair_weight_one, pair_weight_two):
    count_of_rows = BASES // PATCH
    coded = base_codes.reshape(count_of_rows, PATCH)
    onehot = (coded[:, :, None] == jnp.arange(4, dtype=jnp.int32)[None, None, :]).astype(jnp.bfloat16).reshape(count_of_rows, 4 * PATCH)
    stem_output = jnp.dot(onehot, stem_weight, preferred_element_type=jnp.float32).astype(jnp.bfloat16)
    padded_rows = jnp.pad(stem_output, ((DILATION_ROWS, DILATION_ROWS), (0, 0))).astype(jnp.float32)
    normalized_rows = row_norm(padded_rows, conv_gain).astype(jnp.bfloat16)
    summed_taps = jnp.zeros((count_of_rows, C1), jnp.float32)
    for row_shift_amount in range(3):
        summed_taps = summed_taps + jnp.dot(normalized_rows[row_shift_amount * DILATION_ROWS:row_shift_amount * DILATION_ROWS + count_of_rows], dilated_conv_weight[row_shift_amount], preferred_element_type=jnp.float32)
    tower = (stem_output.astype(jnp.float32) + jax.nn.gelu(summed_taps)).astype(jnp.bfloat16)
    halved = jnp.maximum(tower[0::2], tower[1::2])
    fine_features = jax.nn.gelu(jnp.dot(halved, widen_weight, preferred_element_type=jnp.float32)).astype(jnp.bfloat16)
    token = lax.optimization_barrier(jnp.mean(fine_features.astype(jnp.float32).reshape(TOKENS, POOL, C2), axis=1)).astype(jnp.bfloat16)
    token_norm = row_norm(token.astype(jnp.float32), token_gain).astype(jnp.bfloat16)
    factors = jnp.dot(token_norm, proj_weight, preferred_element_type=jnp.float32).astype(jnp.bfloat16)
    row_factor = factors[:, :PC].astype(jnp.float32)
    col_factor = factors[:, PC:].astype(jnp.float32)
    position = jnp.arange(TOKENS, dtype=jnp.int32)
    distance = jnp.log1p(jnp.abs(position[:, None] - position[None, :]).astype(jnp.float32)) / math.log(TOKENS)
    pair_start = (row_factor.T[:, :, None] * col_factor.T[:, None, :] + dist_weight[:, None, None] * distance[None, :, :]).astype(jnp.bfloat16)
    act_one = jax.nn.gelu(pair_start.astype(jnp.float32)).astype(jnp.bfloat16)
    pair_mid = (pair_start.astype(jnp.float32) + pair_conv(act_one, pair_weight_one)).astype(jnp.bfloat16)
    act_two = jax.nn.gelu(pair_mid.astype(jnp.float32)).astype(jnp.bfloat16)
    pair_map = (pair_mid.astype(jnp.float32) + pair_conv(act_two, pair_weight_two)).astype(jnp.bfloat16)
    return (fine_features, pair_map)
```

```python
import functools
import math

import jax
import jax.numpy as jnp
from jax import lax
from jax.experimental import pallas as pl
from jax.experimental.pallas import tpu as pltpu
from jax.sharding import PartitionSpec as P

PATCH = 16
POOL = 64
DILATION_ROWS = 4
CHUNKS = 2
MESH = pl.DeviceIdType.MESH
epsilon = 1e-06
f32 = jnp.float32
bf16 = jnp.bfloat16


def round_up(value, unit):
    return -(-value // unit) * unit


def iota(shape, dim):
    return lax.broadcasted_iota(jnp.int32, shape, dim)


def rounded(value):
    return value.astype(bf16).astype(f32)


def dot(a, b):
    return jnp.dot(a, b, preferred_element_type=f32)


def kernel(
    n_seq,
    n_sec,
    codes,
    stem_weight,
    conv_gain,
    dilated_weight,
    widen_weight,
    token_gain,
    proj_weight,
    dist_weight,
    pair_one,
    pair_two,
    fine_out,
    pair_out,
    codes_ext,
    stem_w,
    gain_w,
    dil_w,
    wid_w,
    tgain_w,
    proj_w,
    dist_w,
    one_w,
    two_w,
    stem_scr,
    norm_scr,
    halved,
    fine,
    tokens,
    factors,
    row_fac,
    col_fac,
    dist_scr,
    start_scr,
    act_scr,
    mid_scr,
    act_two_scr,
    load_sem,
    halo_send,
    halo_recv,
    one_send,
    one_recv,
    half_send,
    half_recv,
    tok_send,
    tok_recv,
    fac_send,
    fac_recv,
    out_sem,
):
    count = n_seq * n_sec
    seq, section, chan = lax.axis_index("seq"), lax.axis_index("section"), lax.axis_index("chan")
    pos = seq * n_sec + section
    other = 1 - chan
    code_rows = codes.shape[0]
    half_rows = halved.shape[1]
    rows = 2 * half_rows
    own_width = halved.shape[2]
    tok_count = half_rows // POOL
    total = tok_count * count
    tile_h, tile_w = tok_count * n_sec, tok_count * n_seq
    start_h, start_w = start_scr.shape[0], start_scr.shape[1]
    mid_h, mid_w = mid_scr.shape[0], mid_scr.shape[1]
    pc = start_scr.shape[2]

    def place(index):
        return {"seq": index // n_sec, "section": index % n_sec}

    def each_peer(body):
        if count <= 16:
            for d in range(1, count):
                body(d)
        else:
            lax.fori_loop(1, count, lambda d, c: (body(d), c)[1], 0)

    pairs = [
        (codes, codes_ext.at[pl.ds(8, code_rows)]),
        (stem_weight, stem_w),
        (conv_gain, gain_w),
        (dilated_weight, dil_w),
        (widen_weight, wid_w),
        (token_gain, tgain_w),
        (proj_weight, proj_w),
        (dist_weight, dist_w),
        (pair_one, one_w.at[chan]),
        (pair_two, two_w),
    ]
    loads = [pltpu.make_async_copy(a, b, load_sem.at[i]) for i, (a, b) in enumerate(pairs)]
    l_codes, l_stem, l_gain, l_dil, l_wid, l_tgain, l_proj, l_dist, l_one, l_two = loads
    for load in loads:
        load.start()

    barrier = pltpu.get_barrier_semaphore()
    pl.semaphore_signal(barrier, inc=1, device_id={"chan": other}, device_id_type=MESH)

    def greet(d):
        peer = lax.rem(pos + d, count)
        pl.semaphore_signal(barrier, inc=1, device_id=place(peer), device_id_type=MESH)

    each_peer(greet)
    pl.semaphore_wait(barrier, count)

    to_next = pltpu.make_async_remote_copy(
        src_ref=codes.at[pl.ds(code_rows - 8, 8)],
        dst_ref=codes_ext.at[pl.ds(0, 8)],
        send_sem=halo_send.at[0],
        recv_sem=halo_recv.at[0],
        device_id=place(lax.rem(pos + 1, count)),
        device_id_type=MESH,
    )
    to_prev = pltpu.make_async_remote_copy(
        src_ref=codes.at[pl.ds(0, 8)],
        dst_ref=codes_ext.at[pl.ds(8 + code_rows, 8)],
        send_sem=halo_send.at[1],
        recv_sem=halo_recv.at[1],
        device_id=place(lax.rem(pos + count - 1, count)),
        device_id_type=MESH,
    )
    one_copy = pltpu.make_async_remote_copy(
        src_ref=pair_one,
        dst_ref=one_w.at[chan],
        send_sem=one_send,
        recv_sem=one_recv,
        device_id={"chan": other},
        device_id_type=MESH,
    )
    one_in = pltpu.make_async_remote_copy(
        src_ref=pair_one,
        dst_ref=one_w.at[other],
        send_sem=one_send,
        recv_sem=one_recv,
        device_id={"chan": other},
        device_id_type=MESH,
    )
    first, last = pos == 0, pos == count - 1

    @pl.when(jnp.logical_not(last))
    def _():
        to_next.start()

    @pl.when(jnp.logical_not(first))
    def _():
        to_prev.start()

    one_copy.start()

    row_anchor, col_anchor = seq * tile_h, section * tile_w
    row_fac[...] = jnp.zeros_like(row_fac)
    col_fac[...] = jnp.zeros_like(col_fac)
    l_dist.wait()
    weight = dist_w[...]
    col_index = col_anchor - 2 + iota((start_w, pc), 0)
    for i in range(start_h):
        gap = jnp.abs(col_index - (row_anchor - 2 + i)).astype(f32)
        dist_scr[i] = jnp.log1p(gap) / math.log(total) * weight

    @pl.when(first)
    def _():
        codes_ext[pl.ds(0, 8), :] = jnp.zeros((8, codes_ext.shape[1]), jnp.int32)

    @pl.when(jnp.logical_not(first))
    def _():
        to_next.wait_recv()

    @pl.when(last)
    def _():
        codes_ext[pl.ds(8 + code_rows, 8), :] = jnp.zeros((8, codes_ext.shape[1]), jnp.int32)

    @pl.when(jnp.logical_not(last))
    def _():
        to_prev.wait_recv()

    l_codes.wait()
    reach = DILATION_ROWS // 2
    ext = norm_scr.shape[0] // 2
    per_row = codes_ext.shape[1] // PATCH
    shift = 8 * per_row

    def patch_of(shape):
        line = iota(shape, 0)
        odd = (line >= ext).astype(jnp.int32)
        return 2 * (line - ext * odd - reach) + odd

    ext_rows = codes_ext.shape[0]
    lanes = codes_ext.shape[1]
    taken = ((patch_of((2 * ext, ext_rows)) + shift) // per_row) == iota((2 * ext, ext_rows), 1)
    spread = dot(taken.astype(f32).astype(bf16), codes_ext[...].astype(f32).astype(bf16))
    patch = patch_of((2 * ext, lanes))
    mine = (iota((2 * ext, lanes), 1) // PATCH) == ((patch + shift) % per_row)
    spread = jnp.where(mine, spread, 0.0).astype(bf16)
    select = (iota((lanes, 4 * PATCH), 0) % PATCH) == (iota((lanes, 4 * PATCH), 1) // 4)
    code = dot(spread, select.astype(f32).astype(bf16))
    patch = patch_of((2 * ext, 4 * PATCH))
    low = jnp.where(first, 0, -shift)
    high = jnp.where(last, rows, rows + shift)
    letter = (iota((2 * ext, 4 * PATCH), 1) % 4).astype(f32)
    hit = (code == letter) & (patch >= low) & (patch < high)
    onehot = jnp.where(hit, 1.0, 0.0).astype(bf16)

    l_stem.wait()
    l_gain.wait()
    square = jnp.zeros((2 * ext, 1), f32)
    stems = []
    for part in range(2):
        stem = rounded(dot(onehot, stem_w[:, part * own_width : (part + 1) * own_width]))
        stem_scr[part] = stem
        stems.append(stem)
        square = square + jnp.sum(stem * stem, axis=1, keepdims=True)
    scale = lax.rsqrt(square / (2 * own_width) + epsilon)
    for part in range(2):
        cols = slice(part * own_width, (part + 1) * own_width)
        norm_scr[:, cols] = stems[part] * scale * gain_w[:, cols]

    l_dil.wait()
    piece = half_rows // CHUNKS
    half_copies = []
    for c in range(CHUNKS):
        taps = None
        for k in range(3):
            at = c * piece + k * reach
            window = jnp.concatenate(
                [norm_scr[at : at + piece, :], norm_scr[ext + at : ext + at + piece, :]], axis=0
            ).astype(bf16)
            term = dot(window, dil_w[k])
            taps = term if taps is None else taps + term
        at = c * piece + reach
        stem_own = jnp.concatenate(
            [stem_scr[chan, at : at + piece, :], stem_scr[chan, ext + at : ext + at + piece, :]], axis=0
        )
        tower = stem_own + jax.nn.gelu(taps)
        top = jnp.maximum(tower[:piece], tower[piece:]).astype(bf16)
        span = pl.ds(c * piece, piece)
        halved[chan, span, :] = top
        copy = pltpu.make_async_remote_copy(
            src_ref=halved.at[chan, span],
            dst_ref=halved.at[chan, span],
            send_sem=half_send.at[c],
            recv_sem=half_recv.at[c],
            device_id={"chan": other},
            device_id_type=MESH,
        )
        copy.start()
        half_copies.append(copy)

    l_wid.wait()
    pieces = []
    for c in range(CHUNKS):
        span = pl.ds(c * piece, piece)
        own_k = pl.ds(pl.multiple_of(chan * own_width, own_width), own_width)
        other_k = pl.ds(pl.multiple_of(other * own_width, own_width), own_width)
        wide = dot(halved[chan, span, :], wid_w[own_k, :])
        arrival = pltpu.make_async_remote_copy(
            src_ref=halved.at[chan, span],
            dst_ref=halved.at[other, span],
            send_sem=half_send.at[c],
            recv_sem=half_recv.at[c],
            device_id={"chan": other},
            device_id_type=MESH,
        )
        arrival.wait_recv()
        wide = wide + dot(halved[other, span, :], wid_w[other_k, :])
        feature = jax.nn.gelu(wide).astype(bf16)
        fine[span, :] = feature
        feature = feature.astype(f32)
        for t in range(piece // POOL):
            mean = jnp.sum(feature[t * POOL : (t + 1) * POOL], axis=0, keepdims=True) * (1.0 / POOL)
            pieces.append(rounded(mean))
    out_copy = pltpu.make_async_copy(fine, fine_out, out_sem)
    out_copy.start()
    for t in range(tokens.shape[1]):
        value = pieces[t] if t < tok_count else jnp.zeros_like(pieces[0])
        tokens[chan, t : t + 1, :] = value
    tok_copy = pltpu.make_async_remote_copy(
        src_ref=tokens.at[chan],
        dst_ref=tokens.at[chan],
        send_sem=tok_send,
        recv_sem=tok_recv,
        device_id={"chan": other},
        device_id_type=MESH,
    )
    tok_copy.start()
    l_tgain.wait()
    l_proj.wait()
    tok_in = pltpu.make_async_remote_copy(
        src_ref=tokens.at[chan],
        dst_ref=tokens.at[other],
        send_sem=tok_send,
        recv_sem=tok_recv,
        device_id={"chan": other},
        device_id_type=MESH,
    )
    tok_in.wait_recv()
    whole = jnp.concatenate([tokens[0], tokens[1]], axis=1)
    mean_square = jnp.sum(whole * whole, axis=1, keepdims=True) / whole.shape[1]
    token_norm = (whole * lax.rsqrt(mean_square + epsilon) * tgain_w[...]).astype(bf16)
    factor = rounded(dot(token_norm, proj_w[...]))
    factors[pos, 0:tok_count, :] = factor[:tok_count, :pc]
    factors[pos, tok_count : 2 * tok_count, :] = factor[:tok_count, pc:]

    def send_factor(d):
        peer = lax.rem(pos + d, count)
        pltpu.make_async_remote_copy(
            src_ref=factors.at[pos],
            dst_ref=factors.at[pos],
            send_sem=fac_send.at[d],
            recv_sem=fac_recv.at[pos],
            device_id=place(peer),
            device_id_type=MESH,
        ).start()

    each_peer(send_factor)

    def take_factor(d):
        source = lax.rem(pos + count - d, count)
        pltpu.make_async_remote_copy(
            src_ref=factors.at[pos],
            dst_ref=factors.at[source],
            send_sem=fac_send.at[d],
            recv_sem=fac_recv.at[source],
            device_id=place(source),
            device_id_type=MESH,
        ).wait_recv()

    each_peer(take_factor)
    for s in range(count):
        at = 8 + s * tok_count
        row_fac[at : at + tok_count, :] = factors[s, 0:tok_count, :]
        col_fac[at : at + tok_count, :] = factors[s, tok_count : 2 * tok_count, :]

    near = col_fac[pl.ds(pl.multiple_of(col_anchor, 8), start_w + 8), :][6 : 6 + start_w]
    col_in = (col_index >= 0) & (col_index < total)
    for i in range(start_h):
        row_here = row_fac[pl.ds(row_anchor + 6 + i, 1), :]
        begin = rounded(row_here * near + dist_scr[i])
        start_scr[i] = begin
        row_index = jnp.zeros_like(col_index) + (row_anchor - 2 + i)
        inside = col_in & (row_index >= 0) & (row_index < total)
        act_scr[i] = jnp.where(inside, jax.nn.gelu(begin), 0.0)

    one_in.wait_recv()
    l_one.wait()
    windows = [
        act_scr[a : a + mid_h, b : b + mid_w, :].reshape(mid_h * mid_w, pc).astype(bf16)
        for a in range(3)
        for b in range(3)
    ]
    flat = jnp.concatenate(windows, axis=1)
    conv = jnp.concatenate([dot(flat, one_w[0]), dot(flat, one_w[1])], axis=1)
    middle = rounded(start_scr[1 : 1 + mid_h, 1 : 1 + mid_w, :].reshape(mid_h * mid_w, pc) + conv)
    mid_scr[...] = middle.reshape(mid_h, mid_w, pc)
    col_mid = col_anchor - 1 + iota((mid_w, pc), 0)
    col_in = (col_mid >= 0) & (col_mid < total)
    for i in range(mid_h):
        row_index = jnp.zeros_like(col_mid) + (row_anchor - 1 + i)
        inside = col_in & (row_index >= 0) & (row_index < total)
        act_two_scr[i] = jnp.where(inside, jax.nn.gelu(mid_scr[i]), 0.0)

    l_two.wait()
    windows = [
        act_two_scr[a : a + tile_h, b : b + tile_w, :].reshape(tile_h * tile_w, pc).astype(bf16)
        for a in range(3)
        for b in range(3)
    ]
    conv = dot(jnp.concatenate(windows, axis=1), two_w[...])
    middle = mid_scr[1 : 1 + tile_h, 1 : 1 + tile_w, :].reshape(tile_h * tile_w, pc)
    width = conv.shape[1]
    own = jnp.where(chan == 0, middle[:, :width], middle[:, width:])
    pair_out[...] = (own + conv).astype(pair_out.dtype)

    @pl.when(jnp.logical_not(last))
    def _():
        to_next.wait_send()

    @pl.when(jnp.logical_not(first))
    def _():
        to_prev.wait_send()

    one_copy.wait_send()
    for copy in half_copies:
        copy.wait_send()
    tok_copy.wait_send()

    def sent(d):
        pltpu.make_async_remote_copy(
            src_ref=factors.at[pos],
            dst_ref=factors.at[pos],
            send_sem=fac_send.at[d],
            recv_sem=fac_recv.at[pos],
            device_id=place(lax.rem(pos + d, count)),
            device_id_type=MESH,
        ).wait_send()

    each_peer(sent)
    out_copy.wait()


def per_device(
    n_seq,
    n_sec,
    base_codes,
    stem_weight,
    conv_gain,
    dilated_conv_weight,
    widen_weight,
    token_gain,
    proj_weight,
    dist_weight,
    pair_weight_one,
    pair_weight_two,
):
    lanes = 128
    count = n_seq * n_sec
    codes = base_codes.reshape(-1, lanes)
    half_rows = base_codes.shape[0] // PATCH // 2
    channels = stem_weight.shape[1]
    own_width = dilated_conv_weight.shape[2]
    wide = widen_weight.shape[1]
    pc, pc_own = pair_weight_one.shape[2], pair_weight_one.shape[3]
    tok_count = half_rows // POOL
    tile_h, tile_w = tok_count * n_sec, tok_count * n_seq
    mid_h, mid_w = tile_h + 2, round_up(tile_w + 2, 8)
    start_h, start_w = tile_h + 4, round_up(mid_w + 2, 8)
    ext = round_up(half_rows + DILATION_ROWS, 8)
    total = tok_count * count
    one = pair_weight_one.reshape(-1, pc_own)
    two = pair_weight_two.reshape(-1, pc_own)
    gain, tgain, dist = conv_gain[None], token_gain[None], dist_weight[None]
    dma = pltpu.SemaphoreType.DMA
    anywhere = pl.BlockSpec(memory_space=pl.ANY)
    vmem = pltpu.VMEM
    fine, pair = pl.pallas_call(
        functools.partial(kernel, n_seq, n_sec),
        out_shape=(
            jax.ShapeDtypeStruct((half_rows, wide), bf16),
            jax.ShapeDtypeStruct((tile_h * tile_w, pc_own), f32),
        ),
        in_specs=[anywhere] * 10,
        out_specs=(anywhere, pl.BlockSpec(memory_space=pltpu.VMEM)),
        scratch_shapes=[
            vmem((codes.shape[0] + 16, lanes), jnp.int32),
            vmem(stem_weight.shape, bf16),
            vmem(gain.shape, f32),
            vmem(dilated_conv_weight.shape, bf16),
            vmem(widen_weight.shape, bf16),
            vmem(tgain.shape, f32),
            vmem(proj_weight.shape, bf16),
            vmem(dist.shape, f32),
            vmem((2,) + one.shape, bf16),
            vmem(two.shape, bf16),
            vmem((2, 2 * ext, own_width), f32),
            vmem((2 * ext, channels), f32),
            vmem((2, half_rows, own_width), bf16),
            vmem((half_rows, wide), bf16),
            vmem((2, round_up(tok_count, 8), wide), f32),
            vmem((count, 2 * tok_count, pc), f32),
            vmem((total + start_h + 16, pc), f32),
            vmem((total + start_w + 16, pc), f32),
            vmem((start_h, start_w, pc), f32),
            vmem((start_h, start_w, pc), f32),
            vmem((start_h, start_w, pc), f32),
            vmem((mid_h, mid_w, pc), f32),
            vmem((mid_h, mid_w, pc), f32),
            dma((10,)),
            dma((2,)),
            dma((2,)),
            dma,
            dma,
            dma((CHUNKS,)),
            dma((CHUNKS,)),
            dma,
            dma,
            dma((count,)),
            dma((count,)),
            dma,
        ],
        compiler_params=pltpu.CompilerParams(
            collective_id=0, has_side_effects=True, vmem_limit_bytes=48 * 1024 * 1024
        ),
    )(
        codes,
        stem_weight,
        gain,
        dilated_conv_weight,
        widen_weight,
        tgain,
        proj_weight,
        dist,
        one,
        two,
    )
    pair_map = pair.astype(bf16).T.reshape(pc_own, tile_h, tile_w)
    return fine, pair_map


def solution(mesh):
    in_specs = (
        P(("groups", "seq", "section")),
        P(),
        P(),
        P(None, None, "chan"),
        P(None, "chan"),
        P(),
        P(),
        P(),
        P(None, None, None, "chan"),
        P(None, None, None, "chan"),
    )
    out_specs = (P(("groups", "seq", "section"), "chan"), P("chan", ("groups", "seq"), "section"))
    body = functools.partial(per_device, mesh.shape["seq"], mesh.shape["section"])
    return jax.shard_map(
        body, mesh=mesh, in_specs=in_specs, out_specs=out_specs, check_vma=False
    )
```

```python
import functools
import math

import jax
import jax.numpy as jnp
from jax import lax
from jax.experimental import pallas as pl
from jax.experimental.pallas import tpu as pltpu
from jax.sharding import PartitionSpec as P

PATCH = 16
POOL = 64
DILATION_ROWS = 4
CHUNKS = 2
MESH = pl.DeviceIdType.MESH
epsilon = 1e-06
f32 = jnp.float32
bf16 = jnp.bfloat16


def round_up(value, unit):
    return -(-value // unit) * unit


def iota(shape, dim):
    return lax.broadcasted_iota(jnp.int32, shape, dim)


def rounded(value):
    return value.astype(bf16).astype(f32)


def dot(a, b):
    return jnp.dot(a, b, preferred_element_type=f32)


def pair_conv(act, weight, height, width):
    total = None
    for a in range(3):
        for b in range(3):
            window = act[a : a + height, b : b + width, :].reshape(height * width, act.shape[2])
            term = lax.dot_general(
                window.astype(bf16),
                weight[3 * a + b],
                (((1,), (1,)), ((), ())),
                preferred_element_type=f32,
            )
            total = term if total is None else total + term
    return total


def kernel(
    n_seq,
    n_sec,
    codes,
    stem_weight,
    conv_gain,
    dilated_weight,
    widen_weight,
    token_gain,
    proj_weight,
    dist_weight,
    pair_one,
    pair_two,
    fine_out,
    pair_out,
    codes_ext,
    stem_w,
    gain_w,
    dil_w,
    wid_w,
    tgain_w,
    proj_w,
    dist_w,
    one_w,
    two_w,
    stem_scr,
    norm_scr,
    halved,
    fine,
    tokens,
    factors,
    row_fac,
    col_fac,
    dist_scr,
    start_scr,
    act_scr,
    mid_scr,
    act_two_scr,
    load_sem,
    halo_send,
    halo_recv,
    one_send,
    one_recv,
    half_send,
    half_recv,
    tok_send,
    tok_recv,
    fac_send,
    fac_recv,
    out_sem,
):
    count = n_seq * n_sec
    seq, section, chan = lax.axis_index("seq"), lax.axis_index("section"), lax.axis_index("chan")
    pos = seq * n_sec + section
    other = 1 - chan
    code_rows = codes.shape[0]
    half_rows = halved.shape[1]
    rows = 2 * half_rows
    own_width = halved.shape[2]
    tok_count = half_rows // POOL
    total = tok_count * count
    tile_h, tile_w = tok_count * n_sec, tok_count * n_seq
    start_h, start_w = start_scr.shape[0], start_scr.shape[1]
    mid_h, mid_w = mid_scr.shape[0], mid_scr.shape[1]
    pc = start_scr.shape[2]

    def place(index):
        return {"seq": index // n_sec, "section": index % n_sec}

    def each_peer(body):
        if count <= 16:
            for d in range(1, count):
                body(d)
        else:
            lax.fori_loop(1, count, lambda d, c: (body(d), c)[1], 0)

    pc_own = pair_one.shape[1]
    own_out = pl.ds(pl.multiple_of(chan * pc_own, pc_own), pc_own)
    other_out = pl.ds(pl.multiple_of(other * pc_own, pc_own), pc_own)
    pairs = [
        (codes, codes_ext.at[pl.ds(8, code_rows)]),
        (stem_weight, stem_w),
        (conv_gain, gain_w),
        (dilated_weight, dil_w),
        (widen_weight, wid_w),
        (token_gain, tgain_w),
        (proj_weight, proj_w),
        (dist_weight, dist_w),
        (pair_one, one_w.at[:, own_out]),
        (pair_two, two_w),
    ]
    loads = [pltpu.make_async_copy(a, b, load_sem.at[i]) for i, (a, b) in enumerate(pairs)]
    l_codes, l_stem, l_gain, l_dil, l_wid, l_tgain, l_proj, l_dist, l_one, l_two = loads
    for load in loads:
        load.start()

    barrier = pltpu.get_barrier_semaphore()
    pl.semaphore_signal(barrier, inc=1, device_id={"chan": other}, device_id_type=MESH)

    def greet(d):
        peer = lax.rem(pos + d, count)
        pl.semaphore_signal(barrier, inc=1, device_id=place(peer), device_id_type=MESH)

    each_peer(greet)
    row_anchor, col_anchor = seq * tile_h, section * tile_w
    row_fac[...] = jnp.zeros_like(row_fac)
    col_fac[...] = jnp.zeros_like(col_fac)
    l_dist.wait()
    weight = dist_w[...]
    col_index = col_anchor - 2 + iota((start_w, pc), 0)

    def distance(i, carry):
        gap = jnp.abs(col_index - (row_anchor - 2 + i)).astype(f32)
        dist_scr[i] = jnp.log1p(gap) / math.log(total) * weight
        return carry

    lax.fori_loop(0, start_h, distance, 0)

    pl.semaphore_wait(barrier, count)

    to_next = pltpu.make_async_remote_copy(
        src_ref=codes.at[pl.ds(code_rows - 8, 8)],
        dst_ref=codes_ext.at[pl.ds(0, 8)],
        send_sem=halo_send.at[0],
        recv_sem=halo_recv.at[0],
        device_id=place(lax.rem(pos + 1, count)),
        device_id_type=MESH,
    )
    to_prev = pltpu.make_async_remote_copy(
        src_ref=codes.at[pl.ds(0, 8)],
        dst_ref=codes_ext.at[pl.ds(8 + code_rows, 8)],
        send_sem=halo_send.at[1],
        recv_sem=halo_recv.at[1],
        device_id=place(lax.rem(pos + count - 1, count)),
        device_id_type=MESH,
    )
    one_copy = pltpu.make_async_remote_copy(
        src_ref=pair_one,
        dst_ref=one_w.at[:, own_out],
        send_sem=one_send,
        recv_sem=one_recv,
        device_id={"chan": other},
        device_id_type=MESH,
    )
    one_in = pltpu.make_async_remote_copy(
        src_ref=pair_one,
        dst_ref=one_w.at[:, other_out],
        send_sem=one_send,
        recv_sem=one_recv,
        device_id={"chan": other},
        device_id_type=MESH,
    )
    first, last = pos == 0, pos == count - 1

    @pl.when(jnp.logical_not(last))
    def _():
        to_next.start()

    @pl.when(jnp.logical_not(first))
    def _():
        to_prev.start()

    one_copy.start()

    reach = DILATION_ROWS // 2
    ext = norm_scr.shape[0] // 2
    lanes = codes_ext.shape[1]
    per_row = lanes // PATCH
    shift = 8 * per_row
    select = (iota((lanes, 4 * PATCH), 0) % PATCH) == (iota((lanes, 4 * PATCH), 1) // 4)
    select = select.astype(f32).astype(bf16)
    gain_rows = [gain_w.at[pl.ds(r, 1)] for r in range(gain_w.shape[0])]

    def stem_block(line_of, height, source, low, high, store):
        def patch_of(width):
            line = line_of(iota((height, width), 0))
            odd = (line >= ext).astype(jnp.int32)
            return 2 * (line - ext * odd - reach) + odd

        code_row = (patch_of(source.shape[0]) + shift) // per_row - (ext_rows - source.shape[0]) // 2
        taken = code_row == iota((height, source.shape[0]), 1)
        spread = dot(taken.astype(f32).astype(bf16), source.astype(f32).astype(bf16))
        mine = (iota((height, lanes), 1) // PATCH) == ((patch_of(lanes) + shift) % per_row)
        spread = jnp.where(mine, spread, 0.0).astype(bf16)
        code = dot(spread, select)
        patch = patch_of(4 * PATCH)
        letter = (iota((height, 4 * PATCH), 1) % 4).astype(f32)
        hit = (code == letter) & (patch >= low) & (patch < high)
        onehot = jnp.where(hit, 1.0, 0.0).astype(bf16)
        stem = rounded(dot(onehot, stem_w[...]))
        square = jnp.sum(stem * stem, axis=1, keepdims=True)
        scale = lax.rsqrt(square / (2 * own_width) + epsilon)
        gain = jnp.concatenate([row[...] for row in gain_rows], axis=1)
        store(stem, stem * scale * gain)

    ext_rows = codes_ext.shape[0]
    tiles = 3 if (2 * ext) % 24 == 0 else 1
    tile = 2 * ext // tiles
    l_codes.wait()
    l_stem.wait()
    l_gain.wait()

    def inner(t, carry):
        start = t * tile
        span = pl.ds(pl.multiple_of(start, 8), tile)

        def store(stem, norm):
            for part in range(2):
                stem_scr[part, span, :] = stem[:, part * own_width : (part + 1) * own_width]
            norm_scr[span, :] = norm

        inside = codes_ext[pl.ds(8, code_rows), :]
        stem_block(lambda line: line + start, tile, inside, 0, rows, store)
        return carry

    lax.fori_loop(0, tiles, inner, 0)

    @pl.when(first)
    def _():
        codes_ext[pl.ds(0, 8), :] = jnp.zeros((8, codes_ext.shape[1]), jnp.int32)

    @pl.when(jnp.logical_not(first))
    def _():
        to_next.wait_recv()

    @pl.when(last)
    def _():
        codes_ext[pl.ds(8 + code_rows, 8), :] = jnp.zeros((8, codes_ext.shape[1]), jnp.int32)

    @pl.when(jnp.logical_not(last))
    def _():
        to_prev.wait_recv()

    def edge_line(line):
        block = line // 8
        return line % 8 + (block % 2) * (ext - 8) + (block // 2) * ext

    def edge_store(stem, norm):
        for block in range(4):
            at = (block % 2) * (ext - 8) + (block // 2) * ext
            norm_scr[at : at + 8, :] = norm[8 * block : 8 * block + 8]

    low = jnp.where(first, 0, -shift)
    high = jnp.where(last, rows, rows + shift)
    stem_block(edge_line, 32, codes_ext[...], low, high, edge_store)

    l_dil.wait()
    piece = half_rows // CHUNKS

    def half_copy(c, source):
        span = pl.ds(pl.multiple_of(c * piece, piece), piece)
        return pltpu.make_async_remote_copy(
            src_ref=halved.at[chan, span],
            dst_ref=halved.at[source, span],
            send_sem=half_send.at[c],
            recv_sem=half_recv.at[c],
            device_id={"chan": other},
            device_id_type=MESH,
        )

    def convolve(c, carry):
        base = c * piece
        area = pl.ds(pl.multiple_of(base, 8), piece + 8)
        area_odd = pl.ds(pl.multiple_of(ext + base, 8), piece + 8)
        even, odd = norm_scr[area, :], norm_scr[area_odd, :]
        taps = None
        for k in range(3):
            at = k * reach
            window = jnp.concatenate([even[at : at + piece], odd[at : at + piece]], axis=0)
            term = dot(window.astype(bf16), dil_w[k])
            taps = term if taps is None else taps + term
        even, odd = stem_scr[chan, area, :], stem_scr[chan, area_odd, :]
        stem_own = jnp.concatenate([even[reach : reach + piece], odd[reach : reach + piece]], axis=0)
        tower = stem_own + jax.nn.gelu(taps)
        top = jnp.maximum(tower[:piece], tower[piece:]).astype(bf16)
        halved[chan, pl.ds(pl.multiple_of(base, piece), piece), :] = top
        half_copy(c, chan).start()
        return carry

    lax.fori_loop(0, CHUNKS, convolve, 0)

    l_wid.wait()
    own_k = pl.ds(pl.multiple_of(chan * own_width, own_width), own_width)
    other_k = pl.ds(pl.multiple_of(other * own_width, own_width), own_width)
    tokens[chan] = jnp.zeros(tokens.shape[1:], f32)
    per_piece = piece // POOL

    def widen(c, carry):
        span = pl.ds(pl.multiple_of(c * piece, piece), piece)
        wide = dot(halved[chan, span, :], wid_w[own_k, :])
        half_copy(c, other).wait_recv()
        wide = wide + dot(halved[other, span, :], wid_w[other_k, :])
        feature = jax.nn.gelu(wide).astype(bf16)
        fine[span, :] = feature
        feature = feature.astype(f32)
        for t in range(per_piece):
            mean = jnp.sum(feature[t * POOL : (t + 1) * POOL], axis=0, keepdims=True) * (1.0 / POOL)
            tokens[chan, pl.ds(c * per_piece + t, 1), :] = rounded(mean)
        return carry

    lax.fori_loop(0, CHUNKS, widen, 0)
    out_copy = pltpu.make_async_copy(fine, fine_out, out_sem)
    out_copy.start()
    tok_copy = pltpu.make_async_remote_copy(
        src_ref=tokens.at[chan],
        dst_ref=tokens.at[chan],
        send_sem=tok_send,
        recv_sem=tok_recv,
        device_id={"chan": other},
        device_id_type=MESH,
    )
    tok_copy.start()
    l_tgain.wait()
    l_proj.wait()
    tok_in = pltpu.make_async_remote_copy(
        src_ref=tokens.at[chan],
        dst_ref=tokens.at[other],
        send_sem=tok_send,
        recv_sem=tok_recv,
        device_id={"chan": other},
        device_id_type=MESH,
    )
    tok_in.wait_recv()
    whole = jnp.concatenate([tokens[0], tokens[1]], axis=1)
    mean_square = jnp.sum(whole * whole, axis=1, keepdims=True) / whole.shape[1]
    tgain = jnp.concatenate([tgain_w[r : r + 1, :] for r in range(tgain_w.shape[0])], axis=1)
    token_norm = (whole * lax.rsqrt(mean_square + epsilon) * tgain).astype(bf16)
    factor = rounded(dot(token_norm, proj_w[...]))
    factors[pos, 0:tok_count, :] = factor[:tok_count, :pc]
    factors[pos, tok_count : 2 * tok_count, :] = factor[:tok_count, pc:]

    def send_factor(d):
        peer = lax.rem(pos + d, count)
        pltpu.make_async_remote_copy(
            src_ref=factors.at[pos],
            dst_ref=factors.at[pos],
            send_sem=fac_send.at[d],
            recv_sem=fac_recv.at[pos],
            device_id=place(peer),
            device_id_type=MESH,
        ).start()

    each_peer(send_factor)

    def take_factor(d):
        source = lax.rem(pos + count - d, count)
        pltpu.make_async_remote_copy(
            src_ref=factors.at[pos],
            dst_ref=factors.at[source],
            send_sem=fac_send.at[d],
            recv_sem=fac_recv.at[source],
            device_id=place(source),
            device_id_type=MESH,
        ).wait_recv()

    each_peer(take_factor)
    for s in range(count):
        at = 8 + s * tok_count
        row_fac[at : at + tok_count, :] = factors[s, 0:tok_count, :]
        col_fac[at : at + tok_count, :] = factors[s, tok_count : 2 * tok_count, :]

    near = col_fac[pl.ds(pl.multiple_of(col_anchor, 8), start_w + 8), :][6 : 6 + start_w]
    col_in = (col_index >= 0) & (col_index < total)
    for i in range(start_h):
        row_here = row_fac[pl.ds(row_anchor + 6 + i, 1), :]
        begin = rounded(row_here * near + dist_scr[i])
        start_scr[i] = begin
        row_index = jnp.zeros_like(col_index) + (row_anchor - 2 + i)
        inside = col_in & (row_index >= 0) & (row_index < total)
        act_scr[i] = jnp.where(inside, jax.nn.gelu(begin), 0.0)

    one_in.wait_recv()
    l_one.wait()
    conv = pair_conv(act_scr, one_w, mid_h, mid_w)
    middle = rounded(start_scr[1 : 1 + mid_h, 1 : 1 + mid_w, :].reshape(mid_h * mid_w, pc) + conv)
    mid_scr[...] = middle.reshape(mid_h, mid_w, pc)
    col_mid = col_anchor - 1 + iota((mid_w, pc), 0)
    col_in = (col_mid >= 0) & (col_mid < total)
    for i in range(mid_h):
        row_index = jnp.zeros_like(col_mid) + (row_anchor - 1 + i)
        inside = col_in & (row_index >= 0) & (row_index < total)
        act_two_scr[i] = jnp.where(inside, jax.nn.gelu(mid_scr[i]), 0.0)

    l_two.wait()
    conv = pair_conv(act_two_scr, two_w, tile_h, tile_w)
    middle = mid_scr[1 : 1 + tile_h, 1 : 1 + tile_w, :].reshape(tile_h * tile_w, pc)
    width = conv.shape[1]
    own = jnp.where(chan == 0, middle[:, :width], middle[:, width:])
    pair_out[...] = (own + conv).astype(pair_out.dtype)

    @pl.when(jnp.logical_not(last))
    def _():
        to_next.wait_send()

    @pl.when(jnp.logical_not(first))
    def _():
        to_prev.wait_send()

    one_copy.wait_send()
    for c in range(CHUNKS):
        half_copy(c, chan).wait_send()
    tok_copy.wait_send()

    def sent(d):
        pltpu.make_async_remote_copy(
            src_ref=factors.at[pos],
            dst_ref=factors.at[pos],
            send_sem=fac_send.at[d],
            recv_sem=fac_recv.at[pos],
            device_id=place(lax.rem(pos + d, count)),
            device_id_type=MESH,
        ).wait_send()

    each_peer(sent)
    out_copy.wait()


def per_device(
    n_seq,
    n_sec,
    base_codes,
    stem_weight,
    conv_gain,
    dilated_conv_weight,
    widen_weight,
    token_gain,
    proj_weight,
    dist_weight,
    pair_weight_one,
    pair_weight_two,
):
    lanes = 128
    count = n_seq * n_sec
    codes = base_codes.reshape(-1, lanes)
    half_rows = base_codes.shape[0] // PATCH // 2
    channels = stem_weight.shape[1]
    own_width = dilated_conv_weight.shape[2]
    wide = widen_weight.shape[1]
    pc, pc_own = pair_weight_one.shape[2], pair_weight_one.shape[3]
    tok_count = half_rows // POOL
    tile_h, tile_w = tok_count * n_sec, tok_count * n_seq
    mid_h, mid_w = tile_h + 2, round_up(tile_w + 2, 8)
    start_h, start_w = tile_h + 4, round_up(mid_w + 2, 8)
    ext = round_up(half_rows + DILATION_ROWS, 8)
    total = tok_count * count
    one = pair_weight_one.transpose(0, 1, 3, 2).reshape(-1, pc_own, pc)
    two = pair_weight_two.transpose(0, 1, 3, 2).reshape(-1, pc_own, pc)
    gain, tgain = conv_gain.reshape(-1, lanes), token_gain.reshape(-1, lanes)
    dist = dist_weight[None]
    dma = pltpu.SemaphoreType.DMA
    anywhere = pl.BlockSpec(memory_space=pltpu.HBM)
    vmem = pltpu.VMEM
    fine, pair = pl.pallas_call(
        functools.partial(kernel, n_seq, n_sec),
        out_shape=(
            jax.ShapeDtypeStruct((half_rows, wide), bf16),
            jax.ShapeDtypeStruct((tile_h * tile_w, pc_own), bf16),
        ),
        in_specs=[anywhere] * 10,
        out_specs=(anywhere, pl.BlockSpec(memory_space=pltpu.VMEM)),
        scratch_shapes=[
            vmem((codes.shape[0] + 16, lanes), jnp.int32),
            vmem(stem_weight.shape, bf16),
            vmem(gain.shape, f32),
            vmem(dilated_conv_weight.shape, bf16),
            vmem(widen_weight.shape, bf16),
            vmem(tgain.shape, f32),
            vmem(proj_weight.shape, bf16),
            vmem(dist.shape, f32),
            vmem((one.shape[0], pc, pc), bf16),
            vmem(two.shape, bf16),
            vmem((2, 2 * ext, own_width), f32),
            vmem((2 * ext, channels), f32),
            vmem((2, half_rows, own_width), bf16),
            vmem((half_rows, wide), bf16),
            vmem((2, round_up(tok_count, 8), wide), f32),
            vmem((count, 2 * tok_count, pc), f32),
            vmem((total + start_h + 16, pc), f32),
            vmem((total + start_w + 16, pc), f32),
            vmem((start_h, start_w, pc), f32),
            vmem((start_h, start_w, pc), f32),
            vmem((start_h, start_w, pc), f32),
            vmem((mid_h, mid_w, pc), f32),
            vmem((mid_h, mid_w, pc), f32),
            dma((10,)),
            dma((2,)),
            dma((2,)),
            dma,
            dma,
            dma((CHUNKS,)),
            dma((CHUNKS,)),
            dma,
            dma,
            dma((count,)),
            dma((count,)),
            dma,
        ],
        compiler_params=pltpu.CompilerParams(
            collective_id=0, has_side_effects=True, vmem_limit_bytes=64 * 1024 * 1024 - 65536
        ),
    )(
        codes,
        stem_weight,
        gain,
        dilated_conv_weight,
        widen_weight,
        tgain,
        proj_weight,
        dist,
        one,
        two,
    )
    pair_map = pair.T.reshape(pc_own, tile_h, tile_w)
    return fine, pair_map


def solution(mesh):
    in_specs = (
        P(("groups", "seq", "section")),
        P(),
        P(),
        P(None, None, "chan"),
        P(None, "chan"),
        P(),
        P(),
        P(),
        P(None, None, None, "chan"),
        P(None, None, None, "chan"),
    )
    out_specs = (P(("groups", "seq", "section"), "chan"), P("chan", ("groups", "seq"), "section"))
    body = functools.partial(per_device, mesh.shape["seq"], mesh.shape["section"])
    return jax.shard_map(
        body, mesh=mesh, in_specs=in_specs, out_specs=out_specs, check_vma=False
    )
```

```python
import functools
import math

import jax
import jax.numpy as jnp
from jax import lax
from jax.experimental import pallas as pl
from jax.experimental.pallas import tpu as pltpu
from jax.sharding import PartitionSpec as P

PATCH = 16
POOL = 64
DILATION_ROWS = 4
CHUNKS = 2
LANES_A = 8
MESH = pl.DeviceIdType.MESH
epsilon = 1e-06
f32 = jnp.float32
bf16 = jnp.bfloat16


def round_up(value, unit):
    return -(-value // unit) * unit


def iota(shape, dim):
    return lax.broadcasted_iota(jnp.int32, shape, dim)


def rounded(value):
    return value.astype(bf16).astype(f32)


def dot(a, b):
    return jnp.dot(a, b, preferred_element_type=f32)


def pair_conv(act, weight, height, width):
    total = None
    for a in range(3):
        for b in range(3):
            window = act[a : a + height, b : b + width, :].reshape(height * width, act.shape[2])
            term = lax.dot_general(
                window.astype(bf16),
                weight[3 * a + b],
                (((1,), (1,)), ((), ())),
                preferred_element_type=f32,
            )
            total = term if total is None else total + term
    return total


def kernel(
    n_seq,
    n_sec,
    codes,
    stem_weight,
    conv_gain,
    dilated_weight,
    widen_weight,
    token_gain,
    proj_weight,
    dist_weight,
    pair_one,
    pair_two,
    fine_out,
    pair_out,
    codes_own,
    codes_halo,
    stem_w,
    gain_w,
    dil_w,
    wid_w,
    tgain_w,
    proj_w,
    dist_w,
    one_w,
    two_w,
    stem_scr,
    norm_scr,
    halved,
    fine,
    tokens,
    factors,
    row_fac,
    col_fac,
    dist_scr,
    start_scr,
    act_scr,
    mid_scr,
    act_two_scr,
    load_sem,
    halo_send,
    halo_recv,
    one_send,
    one_recv,
    half_send,
    half_recv,
    tok_send,
    tok_recv,
    fac_send,
    fac_recv,
):
    count = n_seq * n_sec
    seq, section, chan = lax.axis_index("seq"), lax.axis_index("section"), lax.axis_index("chan")
    pos = seq * n_sec + section
    other = 1 - chan
    code_rows = codes.shape[0]
    half_rows = halved.shape[1]
    rows = 2 * half_rows
    own_width = halved.shape[2]
    tok_count = half_rows // POOL
    total = tok_count * count
    tile_h, tile_w = tok_count * n_sec, tok_count * n_seq
    start_h, start_w = start_scr.shape[0], start_scr.shape[1]
    mid_h, mid_w = mid_scr.shape[0], mid_scr.shape[1]
    pc = start_scr.shape[2]

    def place(index):
        return {"seq": index // n_sec, "section": index % n_sec}

    def each_peer(body):
        if count <= 16:
            for d in range(1, count):
                body(d)
        else:
            lax.fori_loop(1, count, lambda d, c: (body(d), c)[1], 0)

    pc_own = pair_one.shape[1]
    own_out = pl.ds(pl.multiple_of(chan * pc_own, pc_own), pc_own)
    other_out = pl.ds(pl.multiple_of(other * pc_own, pc_own), pc_own)
    pairs = [
        (codes, codes_own),
        (stem_weight, stem_w),
        (conv_gain, gain_w),
        (dilated_weight, dil_w),
        (widen_weight, wid_w),
        (token_gain, tgain_w),
        (proj_weight, proj_w),
        (dist_weight, dist_w),
        (pair_one, one_w.at[:, own_out]),
        (pair_two, two_w),
    ]
    loads = [pltpu.make_async_copy(a, b, load_sem.at[i]) for i, (a, b) in enumerate(pairs)]
    l_codes, l_stem, l_gain, l_dil, l_wid, l_tgain, l_proj, l_dist, l_one, l_two = loads
    for load in loads:
        load.start()

    barrier = pltpu.get_barrier_semaphore()
    pl.semaphore_signal(barrier, inc=1, device_id={"chan": other}, device_id_type=MESH)

    def greet(d):
        peer = lax.rem(pos + d, count)
        pl.semaphore_signal(barrier, inc=1, device_id=place(peer), device_id_type=MESH)

    each_peer(greet)
    row_anchor, col_anchor = seq * tile_h, section * tile_w
    row_fac[...] = jnp.zeros_like(row_fac)
    col_fac[...] = jnp.zeros_like(col_fac)
    l_dist.wait()
    weight = dist_w[...]
    col_index = col_anchor - 2 + iota((start_w, pc), 0)

    def distance(i, carry):
        gap = jnp.abs(col_index - (row_anchor - 2 + i)).astype(f32)
        dist_scr[i] = jnp.log1p(gap) / math.log(total) * weight
        return carry

    lax.fori_loop(0, start_h, distance, 0)

    pl.semaphore_wait(barrier, count)

    to_next = pltpu.make_async_remote_copy(
        src_ref=codes.at[pl.ds(code_rows - 8, 8)],
        dst_ref=codes_halo.at[0],
        send_sem=halo_send.at[0],
        recv_sem=halo_recv.at[0],
        device_id=place(lax.rem(pos + 1, count)),
        device_id_type=MESH,
    )
    to_prev = pltpu.make_async_remote_copy(
        src_ref=codes.at[pl.ds(0, 8)],
        dst_ref=codes_halo.at[1],
        send_sem=halo_send.at[1],
        recv_sem=halo_recv.at[1],
        device_id=place(lax.rem(pos + count - 1, count)),
        device_id_type=MESH,
    )
    one_copy = pltpu.make_async_remote_copy(
        src_ref=pair_one,
        dst_ref=one_w.at[:, own_out],
        send_sem=one_send,
        recv_sem=one_recv,
        device_id={"chan": other},
        device_id_type=MESH,
    )
    one_in = pltpu.make_async_remote_copy(
        src_ref=pair_one,
        dst_ref=one_w.at[:, other_out],
        send_sem=one_send,
        recv_sem=one_recv,
        device_id={"chan": other},
        device_id_type=MESH,
    )
    first, last = pos == 0, pos == count - 1

    @pl.when(jnp.logical_not(last))
    def _():
        to_next.start()

    @pl.when(jnp.logical_not(first))
    def _():
        to_prev.start()

    one_copy.start()

    reach = DILATION_ROWS // 2
    lanes = codes_own.shape[1]
    per_row = lanes // PATCH
    steps = per_row // 2
    groups = code_rows // LANES_A
    line_count = half_rows // LANES_A
    pad = reach * LANES_A
    ext = half_rows + 2 * pad
    letters = 4 * PATCH
    wide_lanes = per_row * lanes
    source = iota((lanes, wide_lanes), 0)
    column = iota((lanes, wide_lanes), 1)
    wanted = (column // lanes) * PATCH + (column % lanes) // 4
    select = ((source == wanted) & (column % lanes < letters)).astype(f32).astype(bf16)

    def coded(parts):
        picked = jnp.concatenate(parts, axis=0)
        code = dot(picked.astype(f32).astype(bf16), select)
        letter = (iota(code.shape, 1) % 4).astype(f32)
        return jnp.where(code == letter, 1.0, 0.0)

    def stem_lines(onehot):
        stem = dot(onehot.astype(bf16), stem_w[...]).astype(bf16)
        value = stem.astype(f32)
        square = jnp.sum(value * value, axis=1, keepdims=True)
        scale = lax.rsqrt(square / (2 * own_width) + epsilon)
        return stem, (value * scale * gain).astype(bf16)

    l_codes.wait()
    l_stem.wait()
    l_gain.wait()
    gain = jnp.concatenate([gain_w[r : r + 1, :] for r in range(gain_w.shape[0])], axis=1)
    own_groups = [codes_own[pl.ds(s, LANES_A, stride=groups), :] for s in range(groups)]
    codes_hot = coded(own_groups)
    for e in range(2):
        blocks = []
        for m in range(line_count):
            group, step = m // steps, m % steps
            at = (2 * step + e) * lanes
            blocks.append(codes_hot[group * LANES_A : (group + 1) * LANES_A, at : at + letters])
        stem, norm = stem_lines(jnp.concatenate(blocks, axis=0))
        for part in range(2):
            stem_scr[part, e * half_rows : (e + 1) * half_rows, :] = stem[
                :, part * own_width : (part + 1) * own_width
            ]
        norm_scr[e * ext + pad : e * ext + pad + half_rows, :] = norm

    @pl.when(first)
    def _():
        codes_halo[0] = jnp.zeros((8, lanes), jnp.int32)

    @pl.when(jnp.logical_not(first))
    def _():
        to_next.wait_recv()

    @pl.when(last)
    def _():
        codes_halo[1] = jnp.zeros((8, lanes), jnp.int32)

    @pl.when(jnp.logical_not(last))
    def _():
        to_prev.wait_recv()

    before = jnp.concatenate([codes_halo[0][7:8], own_groups[groups - 1][: LANES_A - 1]], axis=0)
    after = jnp.concatenate([own_groups[0][1:LANES_A], codes_halo[1][0:1]], axis=0)
    codes_hot = coded([before, after])
    line = iota(codes_hot.shape, 0)
    outside = ((line == 0) & first) | ((line == 2 * LANES_A - 1) & last)
    codes_hot = jnp.where(outside, 0.0, codes_hot)
    blocks = []
    for e in range(2):
        for end, m_list in enumerate((range(steps - reach, steps), range(reach))):
            for step in m_list:
                at = (2 * step + e) * lanes
                blocks.append(codes_hot[end * LANES_A : (end + 1) * LANES_A, at : at + letters])
    _, norm = stem_lines(jnp.concatenate(blocks, axis=0))
    for e in range(2):
        norm_scr[e * ext : e * ext + pad, :] = norm[2 * e * pad : (2 * e + 1) * pad]
        norm_scr[(e + 1) * ext - pad : (e + 1) * ext, :] = norm[(2 * e + 1) * pad : (2 * e + 2) * pad]

    l_dil.wait()
    piece = half_rows // CHUNKS

    def half_copy(c, source):
        span = pl.ds(pl.multiple_of(c * piece, piece), piece)
        return pltpu.make_async_remote_copy(
            src_ref=halved.at[chan, span],
            dst_ref=halved.at[source, span],
            send_sem=half_send.at[c],
            recv_sem=half_recv.at[c],
            device_id={"chan": other},
            device_id_type=MESH,
        )

    def convolve(c, carry):
        base = c * piece
        windows = []
        for k in range(3):
            even = norm_scr[pl.ds(pl.multiple_of(base + k * pad, 16), piece), :]
            odd = norm_scr[pl.ds(pl.multiple_of(ext + base + k * pad, 16), piece), :]
            windows.append(jnp.concatenate([even, odd], axis=0))
        taps = dot(jnp.concatenate(windows, axis=1), dil_w[...].reshape(-1, own_width))
        even = stem_scr[chan, pl.ds(pl.multiple_of(base, 16), piece), :]
        odd = stem_scr[chan, pl.ds(pl.multiple_of(half_rows + base, 16), piece), :]
        stem_own = jnp.concatenate([even, odd], axis=0).astype(f32)
        tower = stem_own + jax.nn.gelu(taps)
        top = jnp.maximum(tower[:piece], tower[piece:]).astype(bf16)
        halved[chan, pl.ds(pl.multiple_of(base, piece), piece), :] = top
        half_copy(c, chan).start()
        return carry

    lax.fori_loop(0, CHUNKS, convolve, 0)

    l_wid.wait()
    own_k = pl.ds(pl.multiple_of(chan * own_width, own_width), own_width)
    other_k = pl.ds(pl.multiple_of(other * own_width, own_width), own_width)

    def widen(c, sums):
        span = pl.ds(pl.multiple_of(c * piece, piece), piece)
        wide = dot(halved[chan, span, :], wid_w[own_k, :])
        half_copy(c, other).wait_recv()
        wide = wide + dot(halved[other, span, :], wid_w[other_k, :])
        feature = jax.nn.gelu(wide).astype(bf16)
        fine[span, :] = feature
        stacked = feature.astype(f32).reshape(piece // LANES_A, LANES_A, feature.shape[1])
        return sums + jnp.sum(stacked, axis=0)

    sums = lax.fori_loop(0, CHUNKS, widen, jnp.zeros((LANES_A, fine.shape[1]), f32))
    per_token = LANES_A // tok_count
    tokens[chan] = jnp.zeros(tokens.shape[1:], f32)
    for t in range(tok_count):
        mean = jnp.sum(sums[t * per_token : (t + 1) * per_token], axis=0, keepdims=True) * (1.0 / POOL)
        tokens[chan, t : t + 1, :] = rounded(mean)
    tok_copy = pltpu.make_async_remote_copy(
        src_ref=tokens.at[chan],
        dst_ref=tokens.at[chan],
        send_sem=tok_send,
        recv_sem=tok_recv,
        device_id={"chan": other},
        device_id_type=MESH,
    )
    tok_copy.start()
    natural = iota((half_rows, half_rows), 0)
    position = LANES_A * (natural % line_count) + natural // line_count
    order = (position == iota((half_rows, half_rows), 1)).astype(f32).astype(bf16)
    fine_out[...] = dot(order, fine[...]).astype(bf16)
    l_tgain.wait()
    l_proj.wait()
    tok_in = pltpu.make_async_remote_copy(
        src_ref=tokens.at[chan],
        dst_ref=tokens.at[other],
        send_sem=tok_send,
        recv_sem=tok_recv,
        device_id={"chan": other},
        device_id_type=MESH,
    )
    tok_in.wait_recv()
    whole = jnp.concatenate([tokens[0], tokens[1]], axis=1)
    mean_square = jnp.sum(whole * whole, axis=1, keepdims=True) / whole.shape[1]
    tgain = jnp.concatenate([tgain_w[r : r + 1, :] for r in range(tgain_w.shape[0])], axis=1)
    token_norm = (whole * lax.rsqrt(mean_square + epsilon) * tgain).astype(bf16)
    factor = rounded(dot(token_norm, proj_w[...]))
    factors[pos, 0:tok_count, :] = factor[:tok_count, :pc]
    factors[pos, tok_count : 2 * tok_count, :] = factor[:tok_count, pc:]

    def send_factor(d):
        peer = lax.rem(pos + d, count)
        pltpu.make_async_remote_copy(
            src_ref=factors.at[pos],
            dst_ref=factors.at[pos],
            send_sem=fac_send.at[d],
            recv_sem=fac_recv.at[pos],
            device_id=place(peer),
            device_id_type=MESH,
        ).start()

    each_peer(send_factor)

    def take_factor(d):
        source = lax.rem(pos + count - d, count)
        pltpu.make_async_remote_copy(
            src_ref=factors.at[pos],
            dst_ref=factors.at[source],
            send_sem=fac_send.at[d],
            recv_sem=fac_recv.at[source],
            device_id=place(source),
            device_id_type=MESH,
        ).wait_recv()

    each_peer(take_factor)
    for s in range(count):
        at = 8 + s * tok_count
        row_fac[at : at + tok_count, :] = factors[s, 0:tok_count, :]
        col_fac[at : at + tok_count, :] = factors[s, tok_count : 2 * tok_count, :]

    near = col_fac[pl.ds(pl.multiple_of(col_anchor, 8), start_w + 8), :][6 : 6 + start_w]
    col_in = (col_index >= 0) & (col_index < total)
    for i in range(start_h):
        row_here = row_fac[pl.ds(row_anchor + 6 + i, 1), :]
        begin = rounded(row_here * near + dist_scr[i])
        start_scr[i] = begin
        row_index = jnp.zeros_like(col_index) + (row_anchor - 2 + i)
        inside = col_in & (row_index >= 0) & (row_index < total)
        act_scr[i] = jnp.where(inside, jax.nn.gelu(begin), 0.0)

    one_in.wait_recv()
    l_one.wait()
    conv = pair_conv(act_scr, one_w, mid_h, mid_w)
    middle = rounded(start_scr[1 : 1 + mid_h, 1 : 1 + mid_w, :].reshape(mid_h * mid_w, pc) + conv)
    mid_scr[...] = middle.reshape(mid_h, mid_w, pc)
    col_mid = col_anchor - 1 + iota((mid_w, pc), 0)
    col_in = (col_mid >= 0) & (col_mid < total)
    for i in range(mid_h):
        row_index = jnp.zeros_like(col_mid) + (row_anchor - 1 + i)
        inside = col_in & (row_index >= 0) & (row_index < total)
        act_two_scr[i] = jnp.where(inside, jax.nn.gelu(mid_scr[i]), 0.0)

    l_two.wait()
    conv = pair_conv(act_two_scr, two_w, tile_h, tile_w)
    middle = mid_scr[1 : 1 + tile_h, 1 : 1 + tile_w, :].reshape(tile_h * tile_w, pc)
    width = conv.shape[1]
    own = jnp.where(chan == 0, middle[:, :width], middle[:, width:])
    pair_out[...] = (own + conv).astype(pair_out.dtype)

    @pl.when(jnp.logical_not(last))
    def _():
        to_next.wait_send()

    @pl.when(jnp.logical_not(first))
    def _():
        to_prev.wait_send()

    one_copy.wait_send()
    for c in range(CHUNKS):
        half_copy(c, chan).wait_send()
    tok_copy.wait_send()

    def sent(d):
        pltpu.make_async_remote_copy(
            src_ref=factors.at[pos],
            dst_ref=factors.at[pos],
            send_sem=fac_send.at[d],
            recv_sem=fac_recv.at[pos],
            device_id=place(lax.rem(pos + d, count)),
            device_id_type=MESH,
        ).wait_send()

    each_peer(sent)


def per_device(
    n_seq,
    n_sec,
    base_codes,
    stem_weight,
    conv_gain,
    dilated_conv_weight,
    widen_weight,
    token_gain,
    proj_weight,
    dist_weight,
    pair_weight_one,
    pair_weight_two,
):
    lanes = 128
    count = n_seq * n_sec
    codes = base_codes.reshape(-1, lanes)
    half_rows = base_codes.shape[0] // PATCH // 2
    channels = stem_weight.shape[1]
    own_width = dilated_conv_weight.shape[2]
    wide = widen_weight.shape[1]
    pc, pc_own = pair_weight_one.shape[2], pair_weight_one.shape[3]
    tok_count = half_rows // POOL
    tile_h, tile_w = tok_count * n_sec, tok_count * n_seq
    mid_h, mid_w = tile_h + 2, round_up(tile_w + 2, 8)
    start_h, start_w = tile_h + 4, round_up(mid_w + 2, 8)
    ext = half_rows + DILATION_ROWS * LANES_A
    total = tok_count * count
    one = pair_weight_one.transpose(0, 1, 3, 2).reshape(-1, pc_own, pc)
    two = pair_weight_two.transpose(0, 1, 3, 2).reshape(-1, pc_own, pc)
    gain, tgain = conv_gain.reshape(-1, lanes), token_gain.reshape(-1, lanes)
    dist = dist_weight[None]
    dma = pltpu.SemaphoreType.DMA
    anywhere = pl.BlockSpec(memory_space=pltpu.HBM)
    vmem = pltpu.VMEM
    fine, pair = pl.pallas_call(
        functools.partial(kernel, n_seq, n_sec),
        out_shape=(
            jax.ShapeDtypeStruct((half_rows, wide), bf16),
            jax.ShapeDtypeStruct((tile_h * tile_w, pc_own), bf16),
        ),
        in_specs=[anywhere] * 10,
        out_specs=(pl.BlockSpec(memory_space=pltpu.VMEM),) * 2,
        scratch_shapes=[
            vmem(codes.shape, jnp.int32),
            vmem((2, 8, lanes), jnp.int32),
            vmem(stem_weight.shape, bf16),
            vmem(gain.shape, f32),
            vmem(dilated_conv_weight.shape, bf16),
            vmem(widen_weight.shape, bf16),
            vmem(tgain.shape, f32),
            vmem(proj_weight.shape, bf16),
            vmem(dist.shape, f32),
            vmem((one.shape[0], pc, pc), bf16),
            vmem(two.shape, bf16),
            vmem((2, 2 * half_rows, own_width), bf16),
            vmem((2 * ext, channels), bf16),
            vmem((2, half_rows, own_width), bf16),
            vmem((half_rows, wide), bf16),
            vmem((2, round_up(tok_count, 8), wide), f32),
            vmem((count, 2 * tok_count, pc), f32),
            vmem((total + start_h + 16, pc), f32),
            vmem((total + start_w + 16, pc), f32),
            vmem((start_h, start_w, pc), f32),
            vmem((start_h, start_w, pc), f32),
            vmem((start_h, start_w, pc), f32),
            vmem((mid_h, mid_w, pc), f32),
            vmem((mid_h, mid_w, pc), f32),
            dma((10,)),
            dma((2,)),
            dma((2,)),
            dma,
            dma,
            dma((CHUNKS,)),
            dma((CHUNKS,)),
            dma,
            dma,
            dma((count,)),
            dma((count,)),
        ],
        compiler_params=pltpu.CompilerParams(
            collective_id=0, has_side_effects=True, vmem_limit_bytes=48 * 1024 * 1024
        ),
    )(
        *(
            pltpu.with_memory_space_constraint(operand, pltpu.HBM)
            for operand in (
                codes,
                stem_weight,
                gain,
                dilated_conv_weight,
                widen_weight,
                tgain,
                proj_weight,
                dist,
                one,
                two,
            )
        )
    )
    pair_map = pair.T.reshape(pc_own, tile_h, tile_w)
    return fine, pair_map


def solution(mesh):
    in_specs = (
        P(("groups", "seq", "section")),
        P(),
        P(),
        P(None, None, "chan"),
        P(None, "chan"),
        P(),
        P(),
        P(),
        P(None, None, None, "chan"),
        P(None, None, None, "chan"),
    )
    out_specs = (P(("groups", "seq", "section"), "chan"), P("chan", ("groups", "seq"), "section"))
    body = functools.partial(per_device, mesh.shape["seq"], mesh.shape["section"])
    return jax.shard_map(
        body, mesh=mesh, in_specs=in_specs, out_specs=out_specs, check_vma=False
    )
```

```python
import functools
import math

import jax
import jax.numpy as jnp
from jax import lax
from jax.experimental import pallas as pl
from jax.experimental.pallas import tpu as pltpu
from jax.sharding import PartitionSpec as P

PATCH = 16
POOL = 64
DILATION_ROWS = 4
CHUNKS = 2
LANES_A = 8
MESH = pl.DeviceIdType.MESH
epsilon = 1e-06
f32 = jnp.float32
bf16 = jnp.bfloat16


def round_up(value, unit):
    return -(-value // unit) * unit


def iota(shape, dim):
    return lax.broadcasted_iota(jnp.int32, shape, dim)


def rounded(value):
    return value.astype(bf16).astype(f32)


def dot(a, b):
    return jnp.dot(a, b, preferred_element_type=f32)


def pair_conv(act, weight, height, width):
    windows = [
        act[a : a + height, b : b + width, :].reshape(height * width, act.shape[2]).astype(bf16)
        for a in range(3)
        for b in range(3)
    ]
    taps = [weight[k] for k in range(9)]
    return lax.dot_general(
        jnp.concatenate(windows, axis=1),
        jnp.concatenate(taps, axis=1),
        (((1,), (1,)), ((), ())),
        preferred_element_type=f32,
    )


def kernel(
    n_seq,
    n_sec,
    codes,
    stem_weight,
    conv_gain,
    dilated_weight,
    widen_weight,
    token_gain,
    proj_weight,
    dist_weight,
    pair_one,
    pair_two,
    fine_out,
    pair_out,
    codes_own,
    codes_halo,
    stem_w,
    gain_w,
    dil_w,
    wid_w,
    tgain_w,
    proj_w,
    dist_w,
    one_w,
    two_w,
    stem_scr,
    norm_scr,
    halved,
    fine,
    tokens,
    factors,
    row_fac,
    col_fac,
    dist_scr,
    start_scr,
    act_scr,
    mid_scr,
    act_two_scr,
    load_sem,
    halo_send,
    halo_recv,
    one_send,
    one_recv,
    half_send,
    half_recv,
    tok_send,
    tok_recv,
    fac_send,
    fac_recv,
):
    count = n_seq * n_sec
    seq, section, chan = lax.axis_index("seq"), lax.axis_index("section"), lax.axis_index("chan")
    pos = seq * n_sec + section
    other = 1 - chan
    code_rows = codes.shape[0]
    half_rows = halved.shape[1]
    rows = 2 * half_rows
    own_width = halved.shape[2]
    tok_count = half_rows // POOL
    total = tok_count * count
    tile_h, tile_w = tok_count * n_sec, tok_count * n_seq
    start_h, start_w = start_scr.shape[0], start_scr.shape[1]
    mid_h, mid_w = mid_scr.shape[0], mid_scr.shape[1]
    pc = start_scr.shape[2]

    def place(index):
        return {"seq": index // n_sec, "section": index % n_sec}

    def each_peer(body):
        if count <= 16:
            for d in sorted(range(1, count), key=lambda d: -min(d, count - d)):
                body(d)
        else:
            lax.fori_loop(1, count, lambda d, c: (body(d), c)[1], 0)

    pc_own = pair_one.shape[1]
    own_out = pl.ds(pl.multiple_of(chan * pc_own, pc_own), pc_own)
    other_out = pl.ds(pl.multiple_of(other * pc_own, pc_own), pc_own)
    pairs = [
        (codes, codes_own),
        (stem_weight, stem_w),
        (conv_gain, gain_w),
        (dilated_weight, dil_w),
        (widen_weight, wid_w),
        (token_gain, tgain_w),
        (proj_weight, proj_w),
        (dist_weight, dist_w),
        (pair_one, one_w.at[:, own_out]),
        (pair_two, two_w),
    ]
    loads = [pltpu.make_async_copy(a, b, load_sem.at[i]) for i, (a, b) in enumerate(pairs)]
    l_codes, l_stem, l_gain, l_dil, l_wid, l_tgain, l_proj, l_dist, l_one, l_two = loads
    barrier = pltpu.get_barrier_semaphore()
    pl.semaphore_signal(barrier, inc=1, device_id={"chan": other}, device_id_type=MESH)

    def greet(d):
        peer = lax.rem(pos + d, count)
        pl.semaphore_signal(barrier, inc=1, device_id=place(peer), device_id_type=MESH)

    each_peer(greet)
    for load in loads:
        load.start()

    pl.semaphore_wait(barrier, count)

    to_next = pltpu.make_async_remote_copy(
        src_ref=codes.at[pl.ds(code_rows - 8, 8)],
        dst_ref=codes_halo.at[0],
        send_sem=halo_send.at[0],
        recv_sem=halo_recv.at[0],
        device_id=place(lax.rem(pos + 1, count)),
        device_id_type=MESH,
    )
    to_prev = pltpu.make_async_remote_copy(
        src_ref=codes.at[pl.ds(0, 8)],
        dst_ref=codes_halo.at[1],
        send_sem=halo_send.at[1],
        recv_sem=halo_recv.at[1],
        device_id=place(lax.rem(pos + count - 1, count)),
        device_id_type=MESH,
    )
    one_copy = pltpu.make_async_remote_copy(
        src_ref=pair_one,
        dst_ref=one_w.at[:, own_out],
        send_sem=one_send,
        recv_sem=one_recv,
        device_id={"chan": other},
        device_id_type=MESH,
    )
    one_in = pltpu.make_async_remote_copy(
        src_ref=pair_one,
        dst_ref=one_w.at[:, other_out],
        send_sem=one_send,
        recv_sem=one_recv,
        device_id={"chan": other},
        device_id_type=MESH,
    )
    first, last = pos == 0, pos == count - 1

    @pl.when(jnp.logical_not(last))
    def _():
        to_next.start()

    @pl.when(jnp.logical_not(first))
    def _():
        to_prev.start()

    one_copy.start()

    reach = DILATION_ROWS // 2
    lanes = codes_own.shape[1]
    per_row = lanes // PATCH
    steps = per_row // 2
    groups = code_rows // LANES_A
    line_count = half_rows // LANES_A
    pad = reach * LANES_A
    ext = half_rows + 2 * pad
    letters = 4 * PATCH
    wide_lanes = per_row * lanes
    source = iota((lanes, wide_lanes), 0)
    column = iota((lanes, wide_lanes), 1)
    wanted = (column // lanes) * PATCH + (column % lanes) // 4
    select = ((source == wanted) & (column % lanes < letters)).astype(f32).astype(bf16)

    def coded(parts):
        picked = jnp.concatenate(parts, axis=0)
        code = dot(picked.astype(f32).astype(bf16), select)
        letter = (iota(code.shape, 1) % 4).astype(f32)
        return jnp.where(code == letter, 1.0, 0.0)

    def stem_lines(onehot):
        stem = dot(onehot.astype(bf16), stem_w[...]).astype(bf16)
        value = stem.astype(f32)
        square = jnp.sum(value * value, axis=1, keepdims=True)
        scale = lax.rsqrt(square / (2 * own_width) + epsilon)
        return stem, (value * scale * gain).astype(bf16)

    l_codes.wait()
    l_stem.wait()
    l_gain.wait()
    gain = jnp.concatenate([gain_w[r : r + 1, :] for r in range(gain_w.shape[0])], axis=1)
    own_groups = [codes_own[pl.ds(s, LANES_A, stride=groups), :] for s in range(groups)]
    codes_hot = coded(own_groups)
    for e in range(2):
        blocks = []
        for m in range(line_count):
            group, step = m // steps, m % steps
            at = (2 * step + e) * lanes
            blocks.append(codes_hot[group * LANES_A : (group + 1) * LANES_A, at : at + letters])
        stem, norm = stem_lines(jnp.concatenate(blocks, axis=0))
        for part in range(2):
            stem_scr[part, e * half_rows : (e + 1) * half_rows, :] = stem[
                :, part * own_width : (part + 1) * own_width
            ]
        norm_scr[e * ext + pad : e * ext + pad + half_rows, :] = norm

    @pl.when(first)
    def _():
        codes_halo[0] = jnp.zeros((8, lanes), jnp.int32)

    @pl.when(jnp.logical_not(first))
    def _():
        to_next.wait_recv()

    @pl.when(last)
    def _():
        codes_halo[1] = jnp.zeros((8, lanes), jnp.int32)

    @pl.when(jnp.logical_not(last))
    def _():
        to_prev.wait_recv()

    before = jnp.concatenate([codes_halo[0][7:8], own_groups[groups - 1][: LANES_A - 1]], axis=0)
    after = jnp.concatenate([own_groups[0][1:LANES_A], codes_halo[1][0:1]], axis=0)
    codes_hot = coded([before, after])
    line = iota(codes_hot.shape, 0)
    outside = ((line == 0) & first) | ((line == 2 * LANES_A - 1) & last)
    codes_hot = jnp.where(outside, 0.0, codes_hot)
    blocks = []
    for e in range(2):
        for end, m_list in enumerate((range(steps - reach, steps), range(reach))):
            for step in m_list:
                at = (2 * step + e) * lanes
                blocks.append(codes_hot[end * LANES_A : (end + 1) * LANES_A, at : at + letters])
    _, norm = stem_lines(jnp.concatenate(blocks, axis=0))
    for e in range(2):
        norm_scr[e * ext : e * ext + pad, :] = norm[2 * e * pad : (2 * e + 1) * pad]
        norm_scr[(e + 1) * ext - pad : (e + 1) * ext, :] = norm[(2 * e + 1) * pad : (2 * e + 2) * pad]

    l_dil.wait()
    piece = half_rows // CHUNKS

    def half_copy(c, source):
        span = pl.ds(pl.multiple_of(c * piece, piece), piece)
        return pltpu.make_async_remote_copy(
            src_ref=halved.at[chan, span],
            dst_ref=halved.at[source, span],
            send_sem=half_send.at[c],
            recv_sem=half_recv.at[c],
            device_id={"chan": other},
            device_id_type=MESH,
        )

    def convolve(c, carry):
        base = c * piece
        windows = []
        for k in range(3):
            even = norm_scr[pl.ds(pl.multiple_of(base + k * pad, 16), piece), :]
            odd = norm_scr[pl.ds(pl.multiple_of(ext + base + k * pad, 16), piece), :]
            windows.append(jnp.concatenate([even, odd], axis=0))
        taps = dot(jnp.concatenate(windows, axis=1), dil_w[...].reshape(-1, own_width))
        even = stem_scr[chan, pl.ds(pl.multiple_of(base, 16), piece), :]
        odd = stem_scr[chan, pl.ds(pl.multiple_of(half_rows + base, 16), piece), :]
        stem_own = jnp.concatenate([even, odd], axis=0).astype(f32)
        tower = stem_own + jax.nn.gelu(taps)
        top = jnp.maximum(tower[:piece], tower[piece:]).astype(bf16)
        halved[chan, pl.ds(pl.multiple_of(base, piece), piece), :] = top
        half_copy(c, chan).start()
        return carry

    lax.fori_loop(0, CHUNKS, convolve, 0)

    l_wid.wait()
    own_k = pl.ds(pl.multiple_of(chan * own_width, own_width), own_width)
    other_k = pl.ds(pl.multiple_of(other * own_width, own_width), own_width)

    def widen(c, sums):
        span = pl.ds(pl.multiple_of(c * piece, piece), piece)
        wide = dot(halved[chan, span, :], wid_w[own_k, :])
        half_copy(c, other).wait_recv()
        wide = wide + dot(halved[other, span, :], wid_w[other_k, :])
        feature = jax.nn.gelu(wide).astype(bf16)
        fine[span, :] = feature
        stacked = feature.astype(f32).reshape(piece // LANES_A, LANES_A, feature.shape[1])
        return sums + jnp.sum(stacked, axis=0)

    sums = lax.fori_loop(0, CHUNKS, widen, jnp.zeros((LANES_A, fine.shape[1]), f32))
    per_token = LANES_A // tok_count
    tokens[chan] = jnp.zeros(tokens.shape[1:], f32)
    for t in range(tok_count):
        mean = jnp.sum(sums[t * per_token : (t + 1) * per_token], axis=0, keepdims=True) * (1.0 / POOL)
        tokens[chan, t : t + 1, :] = rounded(mean)
    tok_copy = pltpu.make_async_remote_copy(
        src_ref=tokens.at[chan],
        dst_ref=tokens.at[chan],
        send_sem=tok_send,
        recv_sem=tok_recv,
        device_id={"chan": other},
        device_id_type=MESH,
    )
    tok_copy.start()
    natural = iota((half_rows, half_rows), 0)
    position = LANES_A * (natural % line_count) + natural // line_count
    order = (position == iota((half_rows, half_rows), 1)).astype(f32).astype(bf16)
    fine_out[...] = dot(order, fine[...]).astype(bf16)
    l_tgain.wait()
    l_proj.wait()
    tok_in = pltpu.make_async_remote_copy(
        src_ref=tokens.at[chan],
        dst_ref=tokens.at[other],
        send_sem=tok_send,
        recv_sem=tok_recv,
        device_id={"chan": other},
        device_id_type=MESH,
    )
    tok_in.wait_recv()
    whole = jnp.concatenate([tokens[0], tokens[1]], axis=1)
    mean_square = jnp.sum(whole * whole, axis=1, keepdims=True) / whole.shape[1]
    tgain = jnp.concatenate([tgain_w[r : r + 1, :] for r in range(tgain_w.shape[0])], axis=1)
    token_norm = (whole * lax.rsqrt(mean_square + epsilon) * tgain).astype(bf16)
    factor = rounded(dot(token_norm, proj_w[...]))
    factors[pos, 0:tok_count, :] = factor[:tok_count, :pc]
    factors[pos, tok_count : 2 * tok_count, :] = factor[:tok_count, pc:]

    def send_factor(d):
        peer = lax.rem(pos + d, count)
        pltpu.make_async_remote_copy(
            src_ref=factors.at[pos],
            dst_ref=factors.at[pos],
            send_sem=fac_send.at[d],
            recv_sem=fac_recv.at[pos],
            device_id=place(peer),
            device_id_type=MESH,
        ).start()

    each_peer(send_factor)
    row_anchor, col_anchor = seq * tile_h, section * tile_w
    row_fac[...] = jnp.zeros_like(row_fac)
    col_fac[...] = jnp.zeros_like(col_fac)
    l_dist.wait()
    weight = dist_w[...]
    col_index = col_anchor - 2 + iota((start_w, pc), 0)

    def distance(i, carry):
        gap = jnp.abs(col_index - (row_anchor - 2 + i)).astype(f32)
        dist_scr[i] = jnp.log1p(gap) / math.log(total) * weight
        return carry

    lax.fori_loop(0, start_h, distance, 0)


    def take_factor(d):
        source = lax.rem(pos + count - d, count)
        pltpu.make_async_remote_copy(
            src_ref=factors.at[pos],
            dst_ref=factors.at[source],
            send_sem=fac_send.at[d],
            recv_sem=fac_recv.at[source],
            device_id=place(source),
            device_id_type=MESH,
        ).wait_recv()

    each_peer(take_factor)
    for s in range(count):
        at = 8 + s * tok_count
        row_fac[at : at + tok_count, :] = factors[s, 0:tok_count, :]
        col_fac[at : at + tok_count, :] = factors[s, tok_count : 2 * tok_count, :]

    near = col_fac[pl.ds(pl.multiple_of(col_anchor, 8), start_w + 8), :][6 : 6 + start_w]
    col_in = (col_index >= 0) & (col_index < total)
    for i in range(start_h):
        row_here = row_fac[pl.ds(row_anchor + 6 + i, 1), :]
        begin = rounded(row_here * near + dist_scr[i])
        start_scr[i] = begin
        row_index = jnp.zeros_like(col_index) + (row_anchor - 2 + i)
        inside = col_in & (row_index >= 0) & (row_index < total)
        act_scr[i] = jnp.where(inside, jax.nn.gelu(begin), 0.0)

    one_in.wait_recv()
    l_one.wait()
    conv = pair_conv(act_scr, one_w, mid_h, mid_w)
    middle = rounded(start_scr[1 : 1 + mid_h, 1 : 1 + mid_w, :].reshape(mid_h * mid_w, pc) + conv)
    mid_scr[...] = middle.reshape(mid_h, mid_w, pc)
    col_mid = col_anchor - 1 + iota((mid_w, pc), 0)
    col_in = (col_mid >= 0) & (col_mid < total)
    for i in range(mid_h):
        row_index = jnp.zeros_like(col_mid) + (row_anchor - 1 + i)
        inside = col_in & (row_index >= 0) & (row_index < total)
        act_two_scr[i] = jnp.where(inside, jax.nn.gelu(mid_scr[i]), 0.0)

    l_two.wait()
    conv = pair_conv(act_two_scr, two_w, tile_h, tile_w)
    middle = mid_scr[1 : 1 + tile_h, 1 : 1 + tile_w, :].reshape(tile_h * tile_w, pc)
    width = conv.shape[1]
    own = jnp.where(chan == 0, middle[:, :width], middle[:, width:])
    pair_out[...] = (own + conv).astype(pair_out.dtype)

    @pl.when(jnp.logical_not(last))
    def _():
        to_next.wait_send()

    @pl.when(jnp.logical_not(first))
    def _():
        to_prev.wait_send()

    one_copy.wait_send()
    for c in range(CHUNKS):
        half_copy(c, chan).wait_send()
    tok_copy.wait_send()

    def sent(d):
        pltpu.make_async_remote_copy(
            src_ref=factors.at[pos],
            dst_ref=factors.at[pos],
            send_sem=fac_send.at[d],
            recv_sem=fac_recv.at[pos],
            device_id=place(lax.rem(pos + d, count)),
            device_id_type=MESH,
        ).wait_send()

    each_peer(sent)


def per_device(
    n_seq,
    n_sec,
    base_codes,
    stem_weight,
    conv_gain,
    dilated_conv_weight,
    widen_weight,
    token_gain,
    proj_weight,
    dist_weight,
    pair_weight_one,
    pair_weight_two,
):
    lanes = 128
    count = n_seq * n_sec
    codes = base_codes.reshape(-1, lanes)
    half_rows = base_codes.shape[0] // PATCH // 2
    channels = stem_weight.shape[1]
    own_width = dilated_conv_weight.shape[2]
    wide = widen_weight.shape[1]
    pc, pc_own = pair_weight_one.shape[2], pair_weight_one.shape[3]
    tok_count = half_rows // POOL
    tile_h, tile_w = tok_count * n_sec, tok_count * n_seq
    mid_h, mid_w = tile_h + 2, round_up(tile_w + 2, 8)
    start_h, start_w = tile_h + 4, round_up(mid_w + 2, 8)
    ext = half_rows + DILATION_ROWS * LANES_A
    total = tok_count * count
    one = pair_weight_one.transpose(0, 1, 3, 2).reshape(-1, pc_own, pc)
    two = pair_weight_two.transpose(0, 1, 3, 2).reshape(-1, pc_own, pc)
    gain, tgain = conv_gain.reshape(-1, lanes), token_gain.reshape(-1, lanes)
    dist = dist_weight[None]
    dma = pltpu.SemaphoreType.DMA
    anywhere = pl.BlockSpec(memory_space=pltpu.HBM)
    vmem = pltpu.VMEM
    fine, pair = pl.pallas_call(
        functools.partial(kernel, n_seq, n_sec),
        out_shape=(
            jax.ShapeDtypeStruct((half_rows, wide), bf16),
            jax.ShapeDtypeStruct((tile_h * tile_w, pc_own), bf16),
        ),
        in_specs=[anywhere] * 10,
        out_specs=(pl.BlockSpec(memory_space=pltpu.VMEM),) * 2,
        scratch_shapes=[
            vmem(codes.shape, jnp.int32),
            vmem((2, 8, lanes), jnp.int32),
            vmem(stem_weight.shape, bf16),
            vmem(gain.shape, f32),
            vmem(dilated_conv_weight.shape, bf16),
            vmem(widen_weight.shape, bf16),
            vmem(tgain.shape, f32),
            vmem(proj_weight.shape, bf16),
            vmem(dist.shape, f32),
            vmem((one.shape[0], pc, pc), bf16),
            vmem(two.shape, bf16),
            vmem((2, 2 * half_rows, own_width), bf16),
            vmem((2 * ext, channels), bf16),
            vmem((2, half_rows, own_width), bf16),
            vmem((half_rows, wide), bf16),
            vmem((2, round_up(tok_count, 8), wide), f32),
            vmem((count, 2 * tok_count, pc), f32),
            vmem((total + start_h + 16, pc), f32),
            vmem((total + start_w + 16, pc), f32),
            vmem((start_h, start_w, pc), f32),
            vmem((start_h, start_w, pc), f32),
            vmem((start_h, start_w, pc), f32),
            vmem((mid_h, mid_w, pc), f32),
            vmem((mid_h, mid_w, pc), f32),
            dma((10,)),
            dma((2,)),
            dma((2,)),
            dma,
            dma,
            dma((CHUNKS,)),
            dma((CHUNKS,)),
            dma,
            dma,
            dma((count,)),
            dma((count,)),
        ],
        compiler_params=pltpu.CompilerParams(
            collective_id=0, has_side_effects=True, vmem_limit_bytes=48 * 1024 * 1024
        ),
    )(
        *(
            pltpu.with_memory_space_constraint(operand, pltpu.HBM)
            for operand in (
                codes,
                stem_weight,
                gain,
                dilated_conv_weight,
                widen_weight,
                tgain,
                proj_weight,
                dist,
                one,
                two,
            )
        )
    )
    pair_map = pair.T.reshape(pc_own, tile_h, tile_w)
    return fine, pair_map


def solution(mesh):
    in_specs = (
        P(("groups", "seq", "section")),
        P(),
        P(),
        P(None, None, "chan"),
        P(None, "chan"),
        P(),
        P(),
        P(),
        P(None, None, None, "chan"),
        P(None, None, None, "chan"),
    )
    out_specs = (P(("groups", "seq", "section"), "chan"), P("chan", ("groups", "seq"), "section"))
    body = functools.partial(per_device, mesh.shape["seq"], mesh.shape["section"])
    return jax.shard_map(
        body, mesh=mesh, in_specs=in_specs, out_specs=out_specs, check_vma=False
    )
```

```python
import functools
import math

import jax
import jax.numpy as jnp
from jax import lax
from jax.experimental import pallas as pl
from jax.experimental.pallas import tpu as pltpu
from jax.sharding import PartitionSpec as P

PATCH = 16
POOL = 64
DILATION_ROWS = 4
CHUNKS = 2
LANES_A = 8
MESH = pl.DeviceIdType.MESH
epsilon = 1e-06
f32 = jnp.float32
bf16 = jnp.bfloat16


def round_up(value, unit):
    return -(-value // unit) * unit


def iota(shape, dim):
    return lax.broadcasted_iota(jnp.int32, shape, dim)


def rounded(value):
    return value.astype(bf16).astype(f32)


def dot(a, b):
    return jnp.dot(a, b, preferred_element_type=f32)


def pair_conv(act, weight, height, width):
    windows = [
        act[a : a + height, b : b + width, :].reshape(height * width, act.shape[2]).astype(bf16)
        for a in range(3)
        for b in range(3)
    ]
    taps = [weight[k] for k in range(9)]
    return lax.dot_general(
        jnp.concatenate(windows, axis=1),
        jnp.concatenate(taps, axis=1),
        (((1,), (1,)), ((), ())),
        preferred_element_type=f32,
    )


def kernel(
    n_seq,
    n_sec,
    codes,
    stem_weight,
    conv_gain,
    dilated_weight,
    widen_weight,
    token_gain,
    proj_weight,
    dist_weight,
    pair_one,
    pair_two,
    fine_out,
    pair_out,
    codes_own,
    codes_halo,
    stem_w,
    gain_w,
    dil_w,
    wid_w,
    tgain_w,
    proj_w,
    dist_w,
    one_w,
    two_w,
    stem_scr,
    norm_scr,
    halved,
    fine,
    tokens,
    factors,
    row_fac,
    col_fac,
    dist_scr,
    start_scr,
    act_scr,
    mid_scr,
    act_two_scr,
    load_sem,
    halo_send,
    halo_recv,
    one_send,
    one_recv,
    half_send,
    half_recv,
    tok_send,
    tok_recv,
    fac_send,
    fac_recv,
):
    count = n_seq * n_sec
    seq, section, chan = lax.axis_index("seq"), lax.axis_index("section"), lax.axis_index("chan")
    pos = seq * n_sec + section
    other = 1 - chan
    code_rows = codes.shape[0]
    half_rows = halved.shape[1]
    rows = 2 * half_rows
    own_width = halved.shape[2]
    tok_count = half_rows // POOL
    total = tok_count * count
    tile_h, tile_w = tok_count * n_sec, tok_count * n_seq
    start_h, start_w = start_scr.shape[0], start_scr.shape[1]
    mid_h, mid_w = mid_scr.shape[0], mid_scr.shape[1]
    pc = start_scr.shape[2]

    def place(index):
        return {"seq": index // n_sec, "section": index % n_sec}

    def each_peer(body):
        if count <= 16:
            for d in sorted(range(1, count), key=lambda d: -min(d, count - d)):
                body(d)
        else:
            lax.fori_loop(1, count, lambda d, c: (body(d), c)[1], 0)

    pc_own = pair_one.shape[1]
    own_out = pl.ds(pl.multiple_of(chan * pc_own, pc_own), pc_own)
    other_out = pl.ds(pl.multiple_of(other * pc_own, pc_own), pc_own)
    pairs = [
        (codes, codes_own),
        (stem_weight, stem_w),
        (conv_gain, gain_w),
        (dilated_weight, dil_w),
        (widen_weight, wid_w),
        (token_gain, tgain_w),
        (proj_weight, proj_w),
        (dist_weight, dist_w),
        (pair_one, one_w.at[:, own_out]),
        (pair_two, two_w),
    ]
    loads = [pltpu.make_async_copy(a, b, load_sem.at[i]) for i, (a, b) in enumerate(pairs)]
    l_codes, l_stem, l_gain, l_dil, l_wid, l_tgain, l_proj, l_dist, l_one, l_two = loads
    barrier = pltpu.get_barrier_semaphore()
    pl.semaphore_signal(barrier, inc=1, device_id={"chan": other}, device_id_type=MESH)

    def greet(d):
        peer = lax.rem(pos + d, count)
        pl.semaphore_signal(barrier, inc=1, device_id=place(peer), device_id_type=MESH)

    each_peer(greet)
    for load in loads:
        load.start()

    pl.semaphore_wait(barrier, count)

    to_next = pltpu.make_async_remote_copy(
        src_ref=codes.at[pl.ds(code_rows - 8, 8)],
        dst_ref=codes_halo.at[0],
        send_sem=halo_send.at[0],
        recv_sem=halo_recv.at[0],
        device_id=place(lax.rem(pos + 1, count)),
        device_id_type=MESH,
    )
    to_prev = pltpu.make_async_remote_copy(
        src_ref=codes.at[pl.ds(0, 8)],
        dst_ref=codes_halo.at[1],
        send_sem=halo_send.at[1],
        recv_sem=halo_recv.at[1],
        device_id=place(lax.rem(pos + count - 1, count)),
        device_id_type=MESH,
    )
    one_copy = pltpu.make_async_remote_copy(
        src_ref=pair_one,
        dst_ref=one_w.at[:, own_out],
        send_sem=one_send,
        recv_sem=one_recv,
        device_id={"chan": other},
        device_id_type=MESH,
    )
    one_in = pltpu.make_async_remote_copy(
        src_ref=pair_one,
        dst_ref=one_w.at[:, other_out],
        send_sem=one_send,
        recv_sem=one_recv,
        device_id={"chan": other},
        device_id_type=MESH,
    )
    first, last = pos == 0, pos == count - 1

    @pl.when(jnp.logical_not(last))
    def _():
        to_next.start()

    @pl.when(jnp.logical_not(first))
    def _():
        to_prev.start()

    one_copy.start()

    reach = DILATION_ROWS // 2
    lanes = codes_own.shape[1]
    per_row = lanes // PATCH
    steps = per_row // 2
    groups = code_rows // LANES_A
    line_count = half_rows // LANES_A
    pad = reach * LANES_A
    ext = half_rows + 2 * pad
    letters = 4 * PATCH
    wide_lanes = per_row * lanes
    source = iota((lanes, wide_lanes), 0)
    column = iota((lanes, wide_lanes), 1)
    wanted = (column // lanes) * PATCH + (column % lanes) // 4
    select = ((source == wanted) & (column % lanes < letters)).astype(f32).astype(bf16)

    def coded(parts):
        picked = jnp.concatenate(parts, axis=0)
        code = dot(picked.astype(f32).astype(bf16), select)
        letter = (iota(code.shape, 1) % 4).astype(f32)
        return jnp.where(code == letter, 1.0, 0.0)

    def stem_lines(onehot):
        stem = dot(onehot.astype(bf16), stem_w[...]).astype(bf16)
        value = stem.astype(f32)
        square = jnp.sum(value * value, axis=1, keepdims=True)
        scale = lax.rsqrt(square / (2 * own_width) + epsilon)
        return stem, (value * scale * gain).astype(bf16)

    l_codes.wait()
    l_stem.wait()
    l_gain.wait()
    gain = jnp.concatenate([gain_w[r : r + 1, :] for r in range(gain_w.shape[0])], axis=1)
    own_groups = [codes_own[pl.ds(s, LANES_A, stride=groups), :] for s in range(groups)]
    codes_hot = coded(own_groups)
    for e in range(2):
        blocks = []
        for m in range(line_count):
            group, step = m // steps, m % steps
            at = (2 * step + e) * lanes
            blocks.append(codes_hot[group * LANES_A : (group + 1) * LANES_A, at : at + letters])
        stem, norm = stem_lines(jnp.concatenate(blocks, axis=0))
        for part in range(2):
            stem_scr[part, e * half_rows : (e + 1) * half_rows, :] = stem[
                :, part * own_width : (part + 1) * own_width
            ]
        norm_scr[e * ext + pad : e * ext + pad + half_rows, :] = norm

    @pl.when(first)
    def _():
        codes_halo[0] = jnp.zeros((8, lanes), jnp.int32)

    @pl.when(jnp.logical_not(first))
    def _():
        to_next.wait_recv()

    @pl.when(last)
    def _():
        codes_halo[1] = jnp.zeros((8, lanes), jnp.int32)

    @pl.when(jnp.logical_not(last))
    def _():
        to_prev.wait_recv()

    before = jnp.concatenate([codes_halo[0][7:8], own_groups[groups - 1][: LANES_A - 1]], axis=0)
    after = jnp.concatenate([own_groups[0][1:LANES_A], codes_halo[1][0:1]], axis=0)
    codes_hot = coded([before, after])
    line = iota(codes_hot.shape, 0)
    outside = ((line == 0) & first) | ((line == 2 * LANES_A - 1) & last)
    codes_hot = jnp.where(outside, 0.0, codes_hot)
    blocks = []
    for e in range(2):
        for end, m_list in enumerate((range(steps - reach, steps), range(reach))):
            for step in m_list:
                at = (2 * step + e) * lanes
                blocks.append(codes_hot[end * LANES_A : (end + 1) * LANES_A, at : at + letters])
    _, norm = stem_lines(jnp.concatenate(blocks, axis=0))
    for e in range(2):
        norm_scr[e * ext : e * ext + pad, :] = norm[2 * e * pad : (2 * e + 1) * pad]
        norm_scr[(e + 1) * ext - pad : (e + 1) * ext, :] = norm[(2 * e + 1) * pad : (2 * e + 2) * pad]

    l_dil.wait()
    piece = half_rows // CHUNKS

    def half_copy(c, source):
        span = pl.ds(pl.multiple_of(c * piece, piece), piece)
        return pltpu.make_async_remote_copy(
            src_ref=halved.at[chan, span],
            dst_ref=halved.at[source, span],
            send_sem=half_send.at[c],
            recv_sem=half_recv.at[c],
            device_id={"chan": other},
            device_id_type=MESH,
        )

    def convolve(c, carry):
        base = c * piece
        windows = []
        for k in range(3):
            even = norm_scr[pl.ds(pl.multiple_of(base + k * pad, 16), piece), :]
            odd = norm_scr[pl.ds(pl.multiple_of(ext + base + k * pad, 16), piece), :]
            windows.append(jnp.concatenate([even, odd], axis=0))
        taps = dot(jnp.concatenate(windows, axis=1), dil_w[...].reshape(-1, own_width))
        even = stem_scr[chan, pl.ds(pl.multiple_of(base, 16), piece), :]
        odd = stem_scr[chan, pl.ds(pl.multiple_of(half_rows + base, 16), piece), :]
        stem_own = jnp.concatenate([even, odd], axis=0).astype(f32)
        tower = stem_own + jax.nn.gelu(taps)
        top = jnp.maximum(tower[:piece], tower[piece:]).astype(bf16)
        halved[chan, pl.ds(pl.multiple_of(base, piece), piece), :] = top
        half_copy(c, chan).start()
        return carry

    lax.fori_loop(0, CHUNKS, convolve, 0)

    l_wid.wait()
    own_k = pl.ds(pl.multiple_of(chan * own_width, own_width), own_width)
    other_k = pl.ds(pl.multiple_of(other * own_width, own_width), own_width)

    def widen(c, sums):
        span = pl.ds(pl.multiple_of(c * piece, piece), piece)
        wide = dot(halved[chan, span, :], wid_w[own_k, :])
        half_copy(c, other).wait_recv()
        wide = wide + dot(halved[other, span, :], wid_w[other_k, :])
        feature = jax.nn.gelu(wide).astype(bf16)
        fine[span, :] = feature
        stacked = feature.astype(f32).reshape(piece // LANES_A, LANES_A, feature.shape[1])
        return sums + jnp.sum(stacked, axis=0)

    sums = lax.fori_loop(0, CHUNKS, widen, jnp.zeros((LANES_A, fine.shape[1]), f32))
    per_token = LANES_A // tok_count
    tokens[chan] = jnp.zeros(tokens.shape[1:], f32)
    for t in range(tok_count):
        mean = jnp.sum(sums[t * per_token : (t + 1) * per_token], axis=0, keepdims=True) * (1.0 / POOL)
        tokens[chan, t : t + 1, :] = rounded(mean)
    tok_copy = pltpu.make_async_remote_copy(
        src_ref=tokens.at[chan],
        dst_ref=tokens.at[chan],
        send_sem=tok_send,
        recv_sem=tok_recv,
        device_id={"chan": other},
        device_id_type=MESH,
    )
    tok_copy.start()
    natural = iota((half_rows, half_rows), 0)
    position = LANES_A * (natural % line_count) + natural // line_count
    order = (position == iota((half_rows, half_rows), 1)).astype(f32).astype(bf16)
    fine_out[...] = dot(order, fine[...]).astype(bf16)
    l_tgain.wait()
    l_proj.wait()
    tok_in = pltpu.make_async_remote_copy(
        src_ref=tokens.at[chan],
        dst_ref=tokens.at[other],
        send_sem=tok_send,
        recv_sem=tok_recv,
        device_id={"chan": other},
        device_id_type=MESH,
    )
    tok_in.wait_recv()
    whole = jnp.concatenate([tokens[0], tokens[1]], axis=1)
    mean_square = jnp.sum(whole * whole, axis=1, keepdims=True) / whole.shape[1]
    tgain = jnp.concatenate([tgain_w[r : r + 1, :] for r in range(tgain_w.shape[0])], axis=1)
    token_norm = (whole * lax.rsqrt(mean_square + epsilon) * tgain).astype(bf16)
    factor = rounded(dot(token_norm, proj_w[...]))
    factors[pos, 0:tok_count, :] = factor[:tok_count, :pc]
    factors[pos, tok_count : 2 * tok_count, :] = factor[:tok_count, pc:]

    def send_factor(d):
        peer = lax.rem(pos + d, count)
        pltpu.make_async_remote_copy(
            src_ref=factors.at[pos],
            dst_ref=factors.at[pos],
            send_sem=fac_send.at[d],
            recv_sem=fac_recv.at[pos],
            device_id=place(peer),
            device_id_type=MESH,
        ).start()

    each_peer(send_factor)
    row_anchor, col_anchor = seq * tile_h, section * tile_w
    row_fac[...] = jnp.zeros_like(row_fac)
    col_fac[...] = jnp.zeros_like(col_fac)
    l_dist.wait()
    offset = iota(dist_scr.shape, 0) - (start_h - 1)
    gap = jnp.abs(offset + (col_anchor - row_anchor)).astype(f32)
    dist_scr[...] = jnp.log1p(gap) / math.log(total) * dist_w[...]
    col_index = col_anchor - 2 + iota((start_w, pc), 0)


    def take_factor(d):
        source = lax.rem(pos + count - d, count)
        pltpu.make_async_remote_copy(
            src_ref=factors.at[pos],
            dst_ref=factors.at[source],
            send_sem=fac_send.at[d],
            recv_sem=fac_recv.at[source],
            device_id=place(source),
            device_id_type=MESH,
        ).wait_recv()

    each_peer(take_factor)
    for s in range(count):
        at = 8 + s * tok_count
        row_fac[at : at + tok_count, :] = factors[s, 0:tok_count, :]
        col_fac[at : at + tok_count, :] = factors[s, tok_count : 2 * tok_count, :]

    near = col_fac[pl.ds(pl.multiple_of(col_anchor, 8), start_w + 8), :][6 : 6 + start_w]
    col_in = (col_index >= 0) & (col_index < total)
    for i in range(start_h):
        row_here = row_fac[pl.ds(row_anchor + 6 + i, 1), :]
        begin = rounded(row_here * near + dist_scr[start_h - 1 - i : start_h - 1 - i + start_w, :])
        start_scr[i] = begin
        row_index = jnp.zeros_like(col_index) + (row_anchor - 2 + i)
        inside = col_in & (row_index >= 0) & (row_index < total)
        act_scr[i] = jnp.where(inside, jax.nn.gelu(begin), 0.0)

    one_in.wait_recv()
    l_one.wait()
    conv = pair_conv(act_scr, one_w, mid_h, mid_w)
    middle = rounded(start_scr[1 : 1 + mid_h, 1 : 1 + mid_w, :].reshape(mid_h * mid_w, pc) + conv)
    mid_scr[...] = middle.reshape(mid_h, mid_w, pc)
    col_mid = col_anchor - 1 + iota((mid_w, pc), 0)
    col_in = (col_mid >= 0) & (col_mid < total)
    for i in range(mid_h):
        row_index = jnp.zeros_like(col_mid) + (row_anchor - 1 + i)
        inside = col_in & (row_index >= 0) & (row_index < total)
        act_two_scr[i] = jnp.where(inside, jax.nn.gelu(mid_scr[i]), 0.0)

    l_two.wait()
    conv = pair_conv(act_two_scr, two_w, tile_h, tile_w)
    middle = mid_scr[1 : 1 + tile_h, 1 : 1 + tile_w, :].reshape(tile_h * tile_w, pc)
    width = conv.shape[1]
    own = jnp.where(chan == 0, middle[:, :width], middle[:, width:])
    pair_out[...] = (own + conv).astype(pair_out.dtype)

    @pl.when(jnp.logical_not(last))
    def _():
        to_next.wait_send()

    @pl.when(jnp.logical_not(first))
    def _():
        to_prev.wait_send()

    one_copy.wait_send()
    for c in range(CHUNKS):
        half_copy(c, chan).wait_send()
    tok_copy.wait_send()

    def sent(d):
        pltpu.make_async_remote_copy(
            src_ref=factors.at[pos],
            dst_ref=factors.at[pos],
            send_sem=fac_send.at[d],
            recv_sem=fac_recv.at[pos],
            device_id=place(lax.rem(pos + d, count)),
            device_id_type=MESH,
        ).wait_send()

    each_peer(sent)


def write_out(fine, pair, fine_out, pair_out, sems):
    first = pltpu.make_async_copy(fine, fine_out, sems.at[0])
    second = pltpu.make_async_copy(pair, pair_out, sems.at[1])
    first.start()
    second.start()
    first.wait()
    second.wait()


def per_device(
    n_seq,
    n_sec,
    base_codes,
    stem_weight,
    conv_gain,
    dilated_conv_weight,
    widen_weight,
    token_gain,
    proj_weight,
    dist_weight,
    pair_weight_one,
    pair_weight_two,
):
    lanes = 128
    count = n_seq * n_sec
    codes = base_codes.reshape(-1, lanes)
    half_rows = base_codes.shape[0] // PATCH // 2
    channels = stem_weight.shape[1]
    own_width = dilated_conv_weight.shape[2]
    wide = widen_weight.shape[1]
    pc, pc_own = pair_weight_one.shape[2], pair_weight_one.shape[3]
    tok_count = half_rows // POOL
    tile_h, tile_w = tok_count * n_sec, tok_count * n_seq
    mid_h, mid_w = tile_h + 2, round_up(tile_w + 2, 8)
    start_h, start_w = tile_h + 4, round_up(mid_w + 2, 8)
    ext = half_rows + DILATION_ROWS * LANES_A
    total = tok_count * count
    one = pair_weight_one.transpose(0, 1, 3, 2).reshape(-1, pc_own, pc)
    two = pair_weight_two.transpose(0, 1, 3, 2).reshape(-1, pc_own, pc)
    gain, tgain = conv_gain.reshape(-1, lanes), token_gain.reshape(-1, lanes)
    dist = dist_weight[None]
    dma = pltpu.SemaphoreType.DMA
    anywhere = pl.BlockSpec(memory_space=pltpu.HBM)
    vmem = pltpu.VMEM
    fine, pair = pl.pallas_call(
        functools.partial(kernel, n_seq, n_sec),
        out_shape=(
            jax.ShapeDtypeStruct((half_rows, wide), bf16),
            jax.ShapeDtypeStruct((tile_h * tile_w, pc_own), bf16),
        ),
        in_specs=[anywhere] * 10,
        out_specs=(pl.BlockSpec(memory_space=pltpu.VMEM),) * 2,
        scratch_shapes=[
            vmem(codes.shape, jnp.int32),
            vmem((2, 8, lanes), jnp.int32),
            vmem(stem_weight.shape, bf16),
            vmem(gain.shape, f32),
            vmem(dilated_conv_weight.shape, bf16),
            vmem(widen_weight.shape, bf16),
            vmem(tgain.shape, f32),
            vmem(proj_weight.shape, bf16),
            vmem(dist.shape, f32),
            vmem((one.shape[0], pc, pc), bf16),
            vmem(two.shape, bf16),
            vmem((2, 2 * half_rows, own_width), bf16),
            vmem((2 * ext, channels), bf16),
            vmem((2, half_rows, own_width), bf16),
            vmem((half_rows, wide), bf16),
            vmem((2, round_up(tok_count, 8), wide), f32),
            vmem((count, 2 * tok_count, pc), f32),
            vmem((total + start_h + 16, pc), f32),
            vmem((total + start_w + 16, pc), f32),
            vmem((start_h + start_w, pc), f32),
            vmem((start_h, start_w, pc), f32),
            vmem((start_h, start_w, pc), f32),
            vmem((mid_h, mid_w, pc), f32),
            vmem((mid_h, mid_w, pc), f32),
            dma((10,)),
            dma((2,)),
            dma((2,)),
            dma,
            dma,
            dma((CHUNKS,)),
            dma((CHUNKS,)),
            dma,
            dma,
            dma((count,)),
            dma((count,)),
        ],
        compiler_params=pltpu.CompilerParams(
            collective_id=0, has_side_effects=True, vmem_limit_bytes=48 * 1024 * 1024
        ),
    )(
        *(
            pltpu.with_memory_space_constraint(operand, pltpu.HBM)
            for operand in (
                codes,
                stem_weight,
                gain,
                dilated_conv_weight,
                widen_weight,
                tgain,
                proj_weight,
                dist,
                one,
                two,
            )
        )
    )
    fine, pair = pl.pallas_call(
        write_out,
        out_shape=(
            jax.ShapeDtypeStruct(fine.shape, bf16),
            jax.ShapeDtypeStruct(pair.shape, bf16),
        ),
        in_specs=[pl.BlockSpec(memory_space=pl.ANY)] * 2,
        out_specs=(anywhere,) * 2,
        scratch_shapes=[dma((2,))],
    )(fine, pair)
    pair_map = pair.T.reshape(pc_own, tile_h, tile_w)
    return fine, pair_map


def solution(mesh):
    in_specs = (
        P(("groups", "seq", "section")),
        P(),
        P(),
        P(None, None, "chan"),
        P(None, "chan"),
        P(),
        P(),
        P(),
        P(None, None, None, "chan"),
        P(None, None, None, "chan"),
    )
    out_specs = (P(("groups", "seq", "section"), "chan"), P("chan", ("groups", "seq"), "section"))
    body = functools.partial(per_device, mesh.shape["seq"], mesh.shape["section"])
    return jax.shard_map(
        body, mesh=mesh, in_specs=in_specs, out_specs=out_specs, check_vma=False
    )
```
